128 devices in a mesh: dp: 8 (over y_hi, x), space: 16 (over z, y_lo, core).
Axes of the slice: x: 4, y: 4 (y_hi: 2, y_lo: 2; y = y_hi * 2 + y_lo), z: 4, core: 2. Of those that a mesh axis runs over, the one named last changes fastest.
Arguments:
- queries: bfloat16 [16, 1024, 1024], P('dp', 'space'), may hold values from -6 to 6
- keys: bfloat16 [16, 1024, 1024], P('dp', 'space'), may hold values from -6 to 6
- values: bfloat16 [16, 1024, 1024], P('dp', 'space'), may hold values from -6 to 6
- cotangent: bfloat16 [16, 1024, 640], P('dp', 'space'), may hold values from -6 to 6
- timesteps: int32 [16], P('dp'), may hold values from 0 to 999
- time_table: float32 [1000, 1024], replicated, may hold values from -0.3 to 0.3
- out_weight: bfloat16 [1024, 1024], replicated, may hold values from -0.1875 to 0.1875
- conv_weight: bfloat16 [1024, 9, 640], replicated, may hold values from -0.0625 to 0.0625
Outputs:
- query_grad: bfloat16 [16, 1024, 1024], P('dp', 'space')
- key_grad: bfloat16 [16, 1024, 1024], P('dp', 'space')
- value_grad: bfloat16 [16, 1024, 1024], P('dp', 'space')
- out_weight_grad: float32 [1024, 1024], P(('dp', 'space'))
- conv_weight_grad: float32 [1024, 9, 640], P(('dp', 'space'))
The draws below stay inside these ranges and needn't reach their ends.
All inputs are finite; a program needn't handle non-finite values.
Results may differ from the reference program's by a relative error of at most 0.013.
The reference program's roundings to bfloat16 on the way (of `weights`, `attended`, `hidden`, `hidden_grad`, `attended_grad` and `score_grad`) count: a program that leaves them out, or rounds other values in their place, can miss the bound.
Values may be sent and summed in bfloat16 or wider, within the bound.
A program may use at most 128 MiB of HBM per device.

```python
import jax
import jax.numpy as jnp
from jax import lax

HEADS = 16
HEAD_DIM = 64
CH = 1024
COUT = 640
TAPS = 9
STEPS = 1000
GRID = 32
BATCH = 16


def draw_queries(key, part):
    key = jax.random.fold_in(key, 7)
    full_shape = (BATCH, GRID * GRID, HEADS * HEAD_DIM)
    drawn = jnp.clip(jax.random.normal(key, full_shape, jnp.float32), -6.0, 6.0)
    return drawn.astype(jnp.bfloat16)


def draw_keys(key, part):
    key = jax.random.fold_in(key, 13)
    full_shape = (BATCH, GRID * GRID, HEADS * HEAD_DIM)
    drawn = jnp.clip(jax.random.normal(key, full_shape, jnp.float32), -6.0, 6.0)
    return drawn.astype(jnp.bfloat16)


def with_ends(values, key, least, largest):
    index_at = [jax.random.randint(jax.random.fold_in(key, axis), (), 0, length) for axis, length in enumerate(values.shape)]
    widest = values.shape.index(max(values.shape))
    beside = index_at[:widest] + [(index_at[widest] + 1) % values.shape[widest]] + index_at[widest + 1:]
    return values.at[tuple(index_at)].set(least).at[tuple(beside)].set(largest)


def steps_of(own_key, dims, cuts, low, top_value):
    gain = 1.0
    for dim, blocks in cuts:
        heights = jax.random.uniform(jax.random.fold_in(jax.random.fold_in(own_key, 6), dim), (blocks,), jnp.float32, low / len(cuts), top_value / len(cuts))
        gain = gain * jnp.repeat(jnp.exp(heights), dims[dim] // blocks).reshape((-1,) + (1,) * (len(dims) - 1 - dim))
    return gain


def scatter_about(key, extent, spread, most, cuts=(), held_as=jnp.bfloat16):
    gain = steps_of(key, extent, cuts, -0.22, 0.18) if cuts else 1.0
    result = jax.random.normal(key, extent, jnp.float32) * spread * gain
    return jnp.minimum(jnp.maximum(result, -most), most).astype(held_as)


def setup_inputs(seed: int = 0) -> dict:
    key_of = jax.random.split(jax.random.key(seed), 9)
    return {
        "queries": draw_queries(jax.random.fold_in(key_of[8], 71), 0),
        "keys": draw_keys(jax.random.fold_in(key_of[8], 71), 0),
        "values": scatter_about(key_of[2], (BATCH, GRID * GRID, CH), 1.0, 6.0, ((0, 8), (1, 16))),
        "cotangent": scatter_about(key_of[3], (BATCH, GRID * GRID, COUT), 1.0, 6.0, ((0, 8), (1, 16))),
        "timesteps": with_ends(jax.random.randint(key_of[4], (BATCH,), 0, STEPS), jax.random.fold_in(key_of[4], 1), 0, STEPS - 1).astype(jnp.int32),
        "time_table": scatter_about(key_of[5], (STEPS, CH), 0.05, 0.3, (), jnp.float32),
        "out_weight": scatter_about(key_of[6], (CH, CH), CH ** -0.5, 0.1875),
        "conv_weight": scatter_about(key_of[7], (CH, TAPS, COUT), (TAPS * CH) ** -0.5, 0.0625),
    }


def split_heads(tensor):
    samples, length = tensor.shape[0], tensor.shape[1]
    return tensor.reshape(samples, length, HEADS, HEAD_DIM).transpose(0, 2, 1, 3).reshape(samples * HEADS, length, HEAD_DIM)


def merge_heads(tensor, samples):
    length = tensor.shape[1]
    return tensor.reshape(samples, HEADS, length, HEAD_DIM).transpose(0, 2, 1, 3).reshape(samples, length, HEADS * HEAD_DIM)


def softmax_rows(query_head, key_head):
    scores = jnp.dot(query_head, key_head.T, preferred_element_type=jnp.float32) * (HEAD_DIM ** -0.5)
    row_top = jnp.max(scores, axis=1, keepdims=True)
    shifted = jnp.exp(scores - row_top)
    return shifted / jnp.sum(shifted, axis=1, keepdims=True)


def attend_one(inputs):
    query_head, key_head, value_head = inputs
    attention = softmax_rows(query_head, key_head)
    return jnp.dot(attention.astype(jnp.bfloat16), value_head, preferred_element_type=jnp.float32).astype(jnp.bfloat16)


def attend_back(inputs):
    query_head, key_head, value_head, out_head, grad_head = inputs
    attention = softmax_rows(query_head, key_head)
    weights = attention.astype(jnp.bfloat16)
    prob_grad = jnp.dot(grad_head, value_head.T, preferred_element_type=jnp.float32)
    row_delta = jnp.sum(grad_head.astype(jnp.float32) * out_head.astype(jnp.float32), axis=1, keepdims=True)
    score_grad = (attention * (prob_grad - row_delta)).astype(jnp.bfloat16)
    score_scale = HEAD_DIM ** -0.5
    query_grad = (jnp.dot(score_grad, key_head, preferred_element_type=jnp.float32) * score_scale).astype(jnp.bfloat16)
    key_grad = (jnp.dot(score_grad.T, query_head, preferred_element_type=jnp.float32) * score_scale).astype(jnp.bfloat16)
    value_grad = jnp.dot(weights.T, grad_head, preferred_element_type=jnp.float32).astype(jnp.bfloat16)
    return query_grad, key_grad, value_grad


def reference(queries, keys, values, cotangent, timesteps, time_table, out_weight, conv_weight):
    samples = queries.shape[0]
    length = queries.shape[1]
    width_heads = HEADS * HEAD_DIM
    query_split = split_heads(queries)
    key_split = split_heads(keys)
    value_split = split_heads(values)
    attended = merge_heads(lax.map(attend_one, (query_split, key_split, value_split)), samples)
    projected = jnp.dot(attended.reshape(-1, width_heads), out_weight, preferred_element_type=jnp.float32)
    projected = projected.reshape(samples, length, CH) + time_table[timesteps][:, None, :]
    hidden = projected.astype(jnp.bfloat16)
    grad_grid = cotangent.reshape(samples, GRID, GRID, COUT)
    grad_pad = jnp.pad(grad_grid, ((0, 0), (1, 1), (1, 1), (0, 0)))
    hidden_pad = jnp.pad(hidden.reshape(samples, GRID, GRID, CH), ((0, 0), (1, 1), (1, 1), (0, 0)))
    grad_flat = cotangent.reshape(-1, COUT)
    hidden_acc = jnp.zeros((samples * length, CH), jnp.float32)
    tap_grads = []
    for row_step in range(3):
        for col_step in range(3):
            tap_index = 3 * row_step + col_step
            grad_slice = grad_pad[:, 2 - row_step:2 - row_step + GRID, 2 - col_step:2 - col_step + GRID].reshape(-1, COUT)
            hidden_acc = hidden_acc + jnp.dot(grad_slice, conv_weight[:, tap_index, :].T, preferred_element_type=jnp.float32)
            hidden_slice = hidden_pad[:, row_step:row_step + GRID, col_step:col_step + GRID].reshape(-1, CH)
            tap_grads.append(jnp.dot(hidden_slice.T, grad_flat, preferred_element_type=jnp.float32))
    conv_weight_grad = jnp.stack(tap_grads, axis=1)
    hidden_grad = hidden_acc.astype(jnp.bfloat16)
    attended_grad = jnp.dot(hidden_grad, out_weight.T, preferred_element_type=jnp.float32).astype(jnp.bfloat16)
    attended_grad = attended_grad.reshape(samples, length, width_heads)
    out_weight_grad = jnp.dot(attended.reshape(-1, width_heads).T, hidden_grad, preferred_element_type=jnp.float32)
    grads = lax.map(attend_back, (query_split, key_split, value_split, split_heads(attended), split_heads(attended_grad)))
    return (merge_heads(grads[0], samples), merge_heads(grads[1], samples), merge_heads(grads[2], samples), out_weight_grad, conv_weight_grad)
```

```python
import jax
import jax.numpy as jnp
from jax import lax
from jax.sharding import PartitionSpec as P

HEAD_DIM = 64
TAPS = 9
GRID = 32


def padded(block, sides, width):
    for axis, dim in sides:
        count = lax.axis_size(axis)
        forward = [(i, i + 1) for i in range(count - 1)]
        backward = [(target, source) for source, target in forward]
        low = lax.ppermute(
            lax.slice_in_dim(block, block.shape[dim] - width, None, axis=dim), axis, forward
        )
        high = lax.ppermute(lax.slice_in_dim(block, 0, width, axis=dim), axis, backward)
        block = jnp.concatenate([low, block, high], axis=dim)
    return block


def on_device(queries, keys, values, cotangent, timesteps, time_table, out_weight, conv_weight):
    samples, local_tokens, width_heads = queries.shape
    channels = out_weight.shape[1]
    out_channels = cotangent.shape[2]
    grid_side = GRID
    rows_here = local_tokens // grid_side
    score_scale = HEAD_DIM ** (-0.5)
    query_heads, key_heads, value_heads = (
        lax.all_to_all(queries, "space", split_axis=2, concat_axis=1, tiled=True),
        lax.all_to_all(keys, "space", split_axis=2, concat_axis=1, tiled=True),
        lax.all_to_all(values, "space", split_axis=2, concat_axis=1, tiled=True),
    )
    length = query_heads.shape[1]
    heads_here = query_heads.shape[2] // HEAD_DIM
    head_shape = (samples, length, heads_here, HEAD_DIM)
    query_four = query_heads.reshape(head_shape)
    key_four = key_heads.reshape(head_shape)
    value_four = value_heads.reshape(head_shape)
    block_rows = min(512, length)
    block_count = length // block_rows

    def to_blocks(tensor):
        return jnp.moveaxis(
            tensor.reshape(samples, block_count, block_rows, heads_here, HEAD_DIM), 1, 0
        )

    def from_blocks(tensor):
        return jnp.moveaxis(tensor, 0, 1).reshape(samples, length, heads_here * HEAD_DIM)

    def forward_block(query_block):
        scores = (
            jnp.einsum("sqhd,skhd->shqk", query_block, key_four, preferred_element_type=jnp.float32)
            * score_scale
        )
        row_top = jnp.max(scores, axis=3, keepdims=True)
        shifted = jnp.exp(scores - row_top)
        row_total = jnp.sum(shifted, axis=3, keepdims=True)
        attention = (shifted / row_total).astype(jnp.bfloat16)
        out_block = jnp.einsum(
            "shqk,skhd->sqhd", attention, value_four, preferred_element_type=jnp.float32
        ).astype(jnp.bfloat16)
        return (out_block, row_top[..., 0] + jnp.log(row_total[..., 0]))

    out_blocks, log_totals = lax.map(forward_block, to_blocks(query_four))
    attended = lax.all_to_all(
        from_blocks(out_blocks), "space", split_axis=1, concat_axis=2, tiled=True
    )
    selector = (
        timesteps[:, None] == jnp.arange(time_table.shape[0], dtype=jnp.int32)[None, :]
    ).astype(jnp.float32)
    time_bias = jnp.dot(selector, time_table, precision=lax.Precision.HIGHEST)
    projected = jnp.einsum("stc,ce->ste", attended, out_weight, preferred_element_type=jnp.float32)
    hidden = (projected + time_bias[:, None, :]).astype(jnp.bfloat16)
    grad_grid = cotangent.reshape(samples, rows_here, grid_side, out_channels)
    grad_ext = padded(grad_grid, (("space", 1),), 1)
    grad_pad = jnp.pad(grad_ext, ((0, 0), (0, 0), (1, 1), (0, 0)))
    grad_shifts = [
        grad_pad[
            :, 2 - row_step : 2 - row_step + rows_here, 2 - col_step : 2 - col_step + grid_side
        ]
        for row_step in range(3)
        for col_step in range(3)
    ]
    grad_stack = jnp.stack(grad_shifts, axis=3).reshape(-1, TAPS * out_channels)
    weight_flat = conv_weight.reshape(channels, TAPS * out_channels)
    hidden_grad = lax.dot_general(
        grad_stack, weight_flat, (((1,), (1,)), ((), ())), preferred_element_type=jnp.float32
    ).astype(jnp.bfloat16)
    groups = lax.axis_size("dp")
    members = lax.axis_size("space")
    slab = channels // (groups * members)
    own = channels // members
    by_owner = hidden.reshape(samples, local_tokens, groups, members, slab)
    by_owner = jnp.moveaxis(by_owner, 3, 2).reshape(samples, local_tokens, channels)
    hidden_own = lax.all_to_all(by_owner, "space", split_axis=2, concat_axis=1, tiled=True)
    cot_all = lax.all_gather(cotangent, "space", axis=1, tiled=True)
    hidden_grid = hidden_own.reshape(samples, grid_side, grid_side, own)
    hidden_pad = jnp.pad(hidden_grid, ((0, 0), (1, 1), (1, 1), (0, 0)))
    hidden_shifts = [
        hidden_pad[:, row_step : row_step + grid_side, col_step : col_step + grid_side]
        for row_step in range(3)
        for col_step in range(3)
    ]
    hidden_stack = jnp.stack(hidden_shifts, axis=3).reshape(-1, TAPS * own)
    conv_grad = lax.dot_general(
        hidden_stack,
        cot_all.reshape(-1, out_channels),
        (((0,), (0,)), ((), ())),
        preferred_element_type=jnp.float32,
    )
    conv_parts = jnp.transpose(
        conv_grad.reshape(TAPS, groups, slab, out_channels).astype(jnp.bfloat16), (1, 0, 2, 3)
    )
    conv_parts = lax.all_to_all(conv_parts, "dp", split_axis=0, concat_axis=0, tiled=True)
    conv_total = jnp.transpose(jnp.sum(conv_parts.astype(jnp.float32), axis=0), (1, 0, 2))
    attended_grad = jnp.einsum(
        "stc,ec->ste",
        hidden_grad.reshape(samples, local_tokens, channels),
        out_weight,
        preferred_element_type=jnp.float32,
    ).astype(jnp.bfloat16)
    hidden_grad_all = lax.all_gather(
        hidden_grad.reshape(samples, local_tokens, channels), "space", axis=1, tiled=True
    )
    out_grad = lax.dot_general(
        from_blocks(out_blocks).reshape(-1, width_heads // members),
        hidden_grad_all.reshape(-1, channels),
        (((0,), (0,)), ((), ())),
        preferred_element_type=jnp.float32,
    )
    out_parts = out_grad.astype(jnp.bfloat16).reshape(groups, slab, channels)
    out_parts = lax.all_to_all(out_parts, "dp", split_axis=0, concat_axis=0, tiled=True)
    out_sum = jnp.sum(out_parts.astype(jnp.float32), axis=0)
    moves = []
    for group in range(groups):
        for member in range(members):
            moves.append((group * members + member, member * groups + group))
    out_total = lax.ppermute(out_sum, ("dp", "space"), moves)
    grad_heads = lax.all_to_all(attended_grad, "space", split_axis=2, concat_axis=1, tiled=True)
    grad_four = grad_heads.reshape(head_shape)

    def backward_block(carried, inputs):
        key_acc, value_acc = carried
        query_block, grad_block, out_block, log_total = inputs
        scores = (
            jnp.einsum("sqhd,skhd->shqk", query_block, key_four, preferred_element_type=jnp.float32)
            * score_scale
        )
        attention = jnp.exp(scores - log_total[..., None])
        weights = attention.astype(jnp.bfloat16)
        value_acc = value_acc + jnp.einsum(
            "shqk,sqhd->skhd", weights, grad_block, preferred_element_type=jnp.float32
        )
        prob_grad = jnp.einsum(
            "sqhd,skhd->shqk", grad_block, value_four, preferred_element_type=jnp.float32
        )
        row_delta = jnp.sum(grad_block.astype(jnp.float32) * out_block.astype(jnp.float32), axis=3)
        row_delta = jnp.transpose(row_delta, (0, 2, 1))
        score_grad = (attention * (prob_grad - row_delta[..., None])).astype(jnp.bfloat16)
        query_block_grad = (
            jnp.einsum("shqk,skhd->sqhd", score_grad, key_four, preferred_element_type=jnp.float32)
            * score_scale
        ).astype(jnp.bfloat16)
        key_acc = key_acc + jnp.einsum(
            "shqk,sqhd->skhd", score_grad, query_block, preferred_element_type=jnp.float32
        )
        return ((key_acc, value_acc), query_block_grad)

    zeros_acc = jnp.zeros(head_shape, jnp.float32)
    (key_acc, value_acc), query_blocks_grad = lax.scan(
        backward_block,
        (zeros_acc, zeros_acc),
        (to_blocks(query_four), to_blocks(grad_four), out_blocks, log_totals),
    )
    query_local = from_blocks(query_blocks_grad)
    key_local = (
        (key_acc * score_scale).astype(jnp.bfloat16).reshape(samples, length, heads_here * HEAD_DIM)
    )
    value_local = value_acc.astype(jnp.bfloat16).reshape(samples, length, heads_here * HEAD_DIM)
    query_grad, key_grad, value_grad = (
        lax.all_to_all(query_local, "space", split_axis=1, concat_axis=2, tiled=True),
        lax.all_to_all(key_local, "space", split_axis=1, concat_axis=2, tiled=True),
        lax.all_to_all(value_local, "space", split_axis=1, concat_axis=2, tiled=True),
    )
    return (query_grad, key_grad, value_grad, out_total, conv_total)


def solution(mesh):
    return jax.shard_map(
        on_device,
        mesh=mesh,
        in_specs=(
            P("dp", "space", None),
            P("dp", "space", None),
            P("dp", "space", None),
            P("dp", "space", None),
            P("dp"),
            P(),
            P(),
            P(),
        ),
        out_specs=(
            P("dp", "space", None),
            P("dp", "space", None),
            P("dp", "space", None),
            P(("dp", "space"), None),
            P(("dp", "space"), None, None),
        ),
        check_vma=False,
    )
```

```python
import jax
import jax.numpy as jnp
from jax import lax
from jax.experimental import pallas as pl
from jax.experimental.pallas import tpu as pltpu
from jax.sharding import PartitionSpec as P

HEAD_DIM = 64
TAPS = 9
GRID = 32
TOKENS = GRID * GRID
PAIR = 2 * HEAD_DIM
DP = 8
SPACE = 16
CHIPS = 8
CH = 1024
COUT = 640
HERE = 64
SLAB = 8
OWN = DP * SLAB
ROWS = 80
BLOCK = 256
SCALE = HEAD_DIM ** (-0.5)
MESH = pl.DeviceIdType.MESH
NT = (((1,), (1,)), ((), ()))
BF = jnp.bfloat16
F32 = jnp.float32


def mm(a, b):
    return jnp.dot(a, b, preferred_element_type=F32)


def mm_nt(a, b):
    return lax.dot_general(a, b, NT, preferred_element_type=F32)


def kernel(
    q_ref, k_ref, v_ref, cot_ref, w_ref, wconv_ref, bias_ref,
    grads_ref, gw_ref, gc_ref,
    qkv, cot_all, w, wconv, wperm, bias_col, km, dom, vt, kt, probs, ot, att, att_tok,
    z, hg_all, hsend, hbuf, lhs, conv_send, conv_recv, do, dv_acc, dk_acc, gh,
    ow, ow_send, ow_recv, ow_sum, ow_out,
    loc, qkv_s, qkv_r, cot_s, cot_r, att_s, att_r, hg_s, hg_r, hid_s, hid_r,
    conv_s, conv_r, ow_s, ow_r, gr_s, gr_r, one_s, one_r,
):
    d = lax.axis_index("dp")
    s = lax.axis_index("space")
    c = lax.div(s, 2)
    k = lax.rem(s, 2)
    lin = d * 2 + k

    def lanes(chip):
        return pl.ds(pl.multiple_of(chip * PAIR, PAIR), PAIR)

    def rows(index, size):
        return pl.ds(pl.multiple_of(index * size, size), size)

    def to(i):
        return lax.rem(s + i, SPACE)

    def frm(i):
        return lax.rem(s + SPACE - i, SPACE)

    def chip_to(i):
        return lax.rem(c + i, CHIPS)

    def chip_frm(i):
        return lax.rem(c + CHIPS - i, CHIPS)

    def each(count, body):
        def step(i, carry):
            body(i)
            return carry

        lax.fori_loop(1, count, step, 0)

    def take(ref, sem):
        pltpu.make_async_copy(ref, ref, sem).wait()

    def remote(src, dst, send, recv, where):
        return pltpu.make_async_remote_copy(
            src_ref=src, dst_ref=dst, send_sem=send, recv_sem=recv,
            device_id=where, device_id_type=MESH,
        )

    local = [
        pltpu.make_async_copy(w_ref, w, loc.at[0]),
        pltpu.make_async_copy(wconv_ref, wconv, loc.at[1]),
        pltpu.make_async_copy(cot_ref.at[k], cot_all.at[rows(k * SPACE + s, HERE)], loc.at[2]),
        pltpu.make_async_copy(q_ref.at[k, :, lanes(c)], qkv.at[0, rows(s, HERE)], loc.at[3]),
        pltpu.make_async_copy(k_ref.at[k, :, lanes(c)], qkv.at[1, rows(s, HERE)], loc.at[4]),
        pltpu.make_async_copy(v_ref.at[k, :, lanes(c)], qkv.at[2, rows(s, HERE)], loc.at[5]),
    ]
    for copy in local:
        copy.start()

    barrier = pltpu.get_barrier_semaphore()

    def greet(i):
        pl.semaphore_signal(barrier, inc=1, device_id={"space": to(i)}, device_id_type=MESH)
        other = lax.rem(lin + i, SPACE)
        pl.semaphore_signal(
            barrier, inc=1,
            device_id={"dp": lax.div(other, 2), "space": c * 2 + lax.rem(other, 2)},
            device_id_type=MESH,
        )

    each(SPACE, greet)
    swap = {"dp": c, "space": lin}

    @pl.when(c != d)
    def _():
        pl.semaphore_signal(barrier, inc=1, device_id=swap, device_id_type=MESH)
        pl.semaphore_wait(barrier, 2 * (SPACE - 1) + 1)

    @pl.when(c == d)
    def _():
        pl.semaphore_wait(barrier, 2 * (SPACE - 1))

    def send_cot(i):
        peer = to(i)
        core = lax.rem(peer, 2)
        remote(
            cot_ref.at[core], cot_all.at[rows(core * SPACE + s, HERE)],
            cot_s.at[i], cot_r.at[i], {"space": peer},
        ).start()

    def send_qkv(i):
        peer = to(i)
        chip = lax.div(peer, 2)
        core = lax.rem(peer, 2)
        for j, ref in enumerate((q_ref, k_ref, v_ref)):
            remote(
                ref.at[core, :, lanes(chip)], qkv.at[j, rows(s, HERE)],
                qkv_s.at[i], qkv_r.at[i], {"space": peer},
            ).start()

    each(SPACE, send_qkv)
    each(SPACE, send_cot)

    local[0].wait()
    bias_here = bias_ref[pl.ds(k, 1), :]
    high = bias_here.astype(BF)
    rest = bias_here - high.astype(F32)
    mid = rest.astype(BF)
    low = (rest - mid.astype(F32)).astype(BF)
    pieces = jnp.concatenate(
        [high.astype(F32), mid.astype(F32), low.astype(F32), jnp.zeros((13, CH), F32)], axis=0
    ).astype(BF)

    def permute(i, carry):
        n = lax.broadcasted_iota(jnp.int32, (BLOCK, CH), 0) + i * BLOCK
        e = lax.broadcasted_iota(jnp.int32, (BLOCK, CH), 1)
        n_chip = lax.shift_right_logical(n, 7)
        n_core = lax.shift_right_logical(n, 6) & 1
        n_dp = lax.shift_right_logical(n, 3) & 7
        target = n_dp * 128 + n_chip * 16 + n_core * 8 + (n & 7)
        pick = jnp.where(e == target, 1.0, 0.0).astype(BF)
        wperm[rows(i, BLOCK), :] = mm_nt(pick, w[...]).astype(BF)
        column = jnp.sum(mm_nt(pick, pieces), axis=1, keepdims=True)
        bias_col[rows(i, BLOCK), :] = jnp.broadcast_to(column, (BLOCK, PAIR))
        return carry

    lax.fori_loop(0, CH // BLOCK, permute, 0)

    for copy in local[3:]:
        copy.wait()
    each(SPACE, lambda i: take(qkv.at[:, rows(frm(i), HERE), :], qkv_r.at[i]))
    first = lax.broadcasted_iota(jnp.int32, (TOKENS, PAIR), 1) < HEAD_DIM
    key = qkv[1]
    km[0] = jnp.where(first, key, jnp.zeros_like(key))
    km[1] = jnp.where(first, jnp.zeros_like(key), key)
    kt[...] = key.astype(F32).T.astype(BF)
    vt[...] = qkv[2].astype(F32).T.astype(BF)

    def forward(i, carry):
        here = rows(i, BLOCK)
        query = qkv[0, here, :] * jnp.asarray(SCALE, BF)
        outs = []
        for h in range(2):
            scores = mm_nt(km[h], query)
            top = jnp.max(scores, axis=0, keepdims=True)
            shifted = jnp.exp(scores - top)
            total = jnp.sum(shifted, axis=0, keepdims=True)
            prob = shifted * (1.0 / total)
            probs[h, :, here] = prob
            outs.append(mm(vt[h * HEAD_DIM : (h + 1) * HEAD_DIM, :], prob.astype(BF)))
        out = jnp.concatenate(outs, axis=0)
        ot[:, here] = out.astype(BF)
        att[here, :] = out.T.astype(BF)
        return carry

    lax.fori_loop(0, TOKENS // BLOCK, forward, 0)

    def send_att(i):
        chip = chip_to(i)
        remote(
            att.at[rows(chip, PAIR)], att_tok.at[:, lanes(c)],
            att_s.at[i], att_r.at[i], {"space": chip * 2 + k},
        ).start()

    each(CHIPS, send_att)
    att_tok[:, lanes(c)] = att[rows(c, PAIR), :]

    local[1].wait()
    local[2].wait()
    each(SPACE, lambda i: take(cot_all.at[rows(k * SPACE + frm(i), HERE)], cot_r.at[i]))
    partner = {"space": c * 2 + 1 - k}
    mine = rows(k, TOKENS)
    cot_copy = remote(cot_all.at[mine], cot_all.at[mine], one_s.at[0], one_r.at[0], partner)
    cot_copy.start()
    z[0:GRID, :] = jnp.zeros((GRID, TAPS * PAIR), F32)
    z[GRID + TOKENS :, :] = jnp.zeros((GRID, TAPS * PAIR), F32)

    def taps(i, carry):
        block = cot_all[pl.ds(pl.multiple_of(k * TOKENS + i * BLOCK, BLOCK), BLOCK), :]
        z[pl.ds(pl.multiple_of(GRID + i * BLOCK, GRID), BLOCK), :] = mm_nt(block, wconv[...])
        return carry

    lax.fori_loop(0, TOKENS // BLOCK, taps, 0)
    column = lax.broadcasted_iota(jnp.int32, (TOKENS, PAIR), 0) & (GRID - 1)
    sums = []
    for col in range(3):
        total = None
        for row in range(3):
            start = 2 * GRID - GRID * row
            at = (3 * row + col) * PAIR
            part = z[start : start + TOKENS, at : at + PAIR]
            total = part if total is None else total + part
        sums.append(total)
    hidden_grad = (
        sums[1]
        + jnp.where(column < GRID - 1, pltpu.roll(sums[0], TOKENS - 1, 0), 0.0)
        + jnp.where(column > 0, pltpu.roll(sums[2], 1, 0), 0.0)
    )
    hg_all[:, lanes(c)] = hidden_grad.astype(BF)

    def send_hg(i):
        remote(
            hg_all.at[:, lanes(c)], hg_all.at[:, lanes(c)],
            hg_s.at[i], hg_r.at[i], {"space": chip_to(i) * 2 + k},
        ).start()

    each(CHIPS, send_hg)

    each(CHIPS, lambda i: take(att_tok.at[:, lanes(chip_frm(i))], att_r.at[i]))
    hsend[...] = (mm_nt(wperm[...], att_tok[...]) + bias_col[...]).astype(BF)

    def send_hidden(i):
        peer = to(i)
        remote(
            hsend.at[rows(peer, OWN)], hbuf.at[:, lanes(k * CHIPS + c)],
            hid_s.at[i], hid_r.at[i], {"space": peer},
        ).start()

    each(SPACE, send_hidden)
    hbuf[:, lanes(k * CHIPS + c)] = hsend[rows(s, OWN), :]

    def take_hidden(i):
        peer = frm(i)
        take(hbuf.at[:, lanes(lax.rem(peer, 2) * CHIPS + lax.div(peer, 2))], hid_r.at[i])

    each(SPACE, take_hidden)
    cot_copy.wait_send()
    take(cot_all.at[rows(1 - k, TOKENS)], one_r.at[0])

    spot = lax.broadcasted_iota(jnp.int32, (OWN, TOKENS), 1)
    y = lax.shift_right_logical(spot, 5)
    x = spot & (GRID - 1)
    for sample in range(2):
        inside = slice(sample * TOKENS, (sample + 1) * TOKENS)
        hidden = hbuf[:, inside].astype(F32)
        for row in range(3):
            for col in range(3):
                offset = (row - 1) * GRID + col - 1
                moved = pltpu.roll(hidden, (-offset) % TOKENS, 1) if offset else hidden
                good = None
                for ok in (
                    [y > 0] * (row == 0) + [y < GRID - 1] * (row == 2)
                    + [x > 0] * (col == 0) + [x < GRID - 1] * (col == 2)
                ):
                    good = ok if good is None else good & ok
                if good is not None:
                    moved = jnp.where(good, moved, 0.0)
                tap = 3 * row + col
                lhs[tap * OWN : (tap + 1) * OWN, inside] = moved.astype(BF)
    lhs[TAPS * OWN :, :] = jnp.zeros((OWN, 2 * TOKENS), BF)
    for at in range(0, COUT, BLOCK):
        end = min(at + BLOCK, COUT)
        part = mm(lhs[...], cot_all[:, at:end])
        for dest in range(DP):
            for pair in range(5):
                top = pair * 2 * OWN + dest * SLAB
                both = jnp.concatenate(
                    [part[top : top + SLAB], part[top + OWN : top + OWN + SLAB]], axis=0
                )
                conv_send[dest, pair * 16 : pair * 16 + 16, at:end] = both.astype(BF)

    def send_conv(i):
        dest = lax.rem(d + i, DP)
        remote(
            conv_send.at[dest], conv_recv.at[i], conv_s.at[i], conv_r.at[i], {"dp": dest}
        ).start()

    each(DP, send_conv)

    each(CHIPS, lambda i: take(hg_all.at[:, lanes(chip_frm(i))], hg_r.at[i]))
    do[...] = mm_nt(hg_all[...], w[rows(c, PAIR), :]).astype(BF)
    grad = do[...]
    dom[0] = jnp.where(first, grad, jnp.zeros_like(grad))
    dom[1] = jnp.where(first, jnp.zeros_like(grad), grad)
    dv_acc[...] = jnp.zeros_like(dv_acc)
    dk_acc[...] = jnp.zeros_like(dk_acc)

    def backward(i, carry):
        here = rows(i, BLOCK)
        query = qkv[0, here, :] * jnp.asarray(SCALE, BF)
        half = lax.broadcasted_iota(jnp.int32, (BLOCK, PAIR), 1) < HEAD_DIM
        product = ot[:, here].astype(F32) * do[here, :].astype(F32).T
        outs = []
        for h in range(2):
            prob = probs[h, :, here]
            grad_block = dom[h, here, :]
            dv_acc[...] += mm(prob.astype(BF), grad_block)
            prob_grad = mm_nt(qkv[2], grad_block)
            delta = jnp.sum(product[h * HEAD_DIM : (h + 1) * HEAD_DIM], axis=0, keepdims=True)
            score_grad = (prob * (prob_grad - delta)).astype(BF)
            zero = jnp.zeros_like(query)
            masked = jnp.where(half, query, zero) if h == 0 else jnp.where(half, zero, query)
            dk_acc[...] += mm(score_grad, masked)
            outs.append(mm(kt[h * HEAD_DIM : (h + 1) * HEAD_DIM, :], score_grad))
        gh[0, here, :] = (jnp.concatenate(outs, axis=0) * SCALE).T.astype(BF)
        return carry

    lax.fori_loop(0, TOKENS // BLOCK, backward, 0)
    gh[1] = dk_acc[...].astype(BF)
    gh[2] = dv_acc[...].astype(BF)

    def send_grads(i):
        peer = to(i)
        remote(
            gh.at[:, rows(peer, HERE), :], grads_ref.at[:, k, :, lanes(c)],
            gr_s.at[i], gr_r.at[i], {"space": peer},
        ).start()

    each(SPACE, send_grads)
    own_grads = pltpu.make_async_copy(
        gh.at[:, rows(s, HERE), :], grads_ref.at[:, k, :, lanes(c)], loc.at[0]
    )
    own_grads.start()

    ow[...] = mm(ot[...], hg_all[...])
    for piece in range(SPACE):
        band = ow[piece * SLAB : (piece + 1) * SLAB, :]
        ow_send[piece] = jnp.concatenate([band[:, : CH // 2], band[:, CH // 2 :]], axis=0).astype(BF)

    def send_ow(i):
        other = lax.rem(lin + i, SPACE)
        remote(
            ow_send.at[other], ow_recv.at[i], ow_s.at[i], ow_r.at[i],
            {"dp": lax.div(other, 2), "space": c * 2 + lax.rem(other, 2)},
        ).start()

    each(SPACE, send_ow)

    each(DP, lambda i: take(conv_recv.at[i], conv_r.at[i]))
    total = conv_send[d].astype(F32)
    for i in range(1, DP):
        total = total + conv_recv[i].astype(F32)
    for tap in range(TAPS):
        gc_ref[tap] = total[tap * SLAB : (tap + 1) * SLAB]

    each(SPACE, lambda i: take(ow_recv.at[i], ow_r.at[i]))
    total = ow_send[lin].astype(F32)
    for i in range(1, SPACE):
        total = total + ow_recv[i].astype(F32)
    ow_sum[:, : CH // 2] = total[:SLAB]
    ow_sum[:, CH // 2 :] = total[SLAB:]

    @pl.when(c != d)
    def _():
        copy = remote(ow_sum, ow_out, one_s.at[1], one_r.at[1], swap)
        copy.start()
        copy.wait()

    @pl.when(c == d)
    def _():
        copy = pltpu.make_async_copy(ow_sum, ow_out, loc.at[1])
        copy.start()
        copy.wait()

    gw_ref[...] = ow_out[...]

    own_grads.wait()

    def take_grads(i):
        peer = frm(i)
        take(grads_ref.at[:, lax.rem(peer, 2), :, lanes(lax.div(peer, 2))], gr_r.at[i])

    each(SPACE, take_grads)

    def sent(i):
        take(qkv.at[:, rows(0, HERE), :], qkv_s.at[i])
        take(cot_all.at[rows(0, HERE)], cot_s.at[i])
        take(hsend.at[rows(0, OWN)], hid_s.at[i])
        take(gh.at[:, rows(0, HERE), :], gr_s.at[i])
        take(ow_send.at[0], ow_s.at[i])

    each(SPACE, sent)

    def sent_chips(i):
        take(att.at[rows(0, PAIR)], att_s.at[i])
        take(hg_all.at[:, lanes(0)], hg_s.at[i])
        take(conv_send.at[0], conv_s.at[i])

    each(CHIPS, sent_chips)


def on_device(queries, keys, values, cotangent, timesteps, time_table, out_weight, conv_weight):
    chip = lax.axis_index("space") // 2
    bias = jnp.concatenate(
        [lax.dynamic_slice(time_table, (timesteps[i], 0), (1, CH)) for i in range(2)], axis=0
    )
    own = lax.dynamic_slice(conv_weight, (chip * PAIR, 0, 0), (PAIR, TAPS, COUT))
    wconv = jnp.transpose(own, (1, 0, 2)).reshape(TAPS * PAIR, COUT)
    anywhere = pl.BlockSpec(memory_space=pl.ANY)
    vmem = pl.BlockSpec(memory_space=pltpu.VMEM)
    sems = pltpu.SemaphoreType.DMA
    grads, gw, gc = pl.pallas_call(
        kernel,
        out_shape=(
            jax.ShapeDtypeStruct((3, 2, HERE, CH), BF),
            jax.ShapeDtypeStruct((SLAB, CH), F32),
            jax.ShapeDtypeStruct((TAPS, SLAB, COUT), F32),
        ),
        in_specs=[anywhere] * 6 + [vmem],
        out_specs=(anywhere, vmem, vmem),
        scratch_shapes=[
            pltpu.VMEM((3, TOKENS, PAIR), BF),
            pltpu.VMEM((2 * TOKENS, COUT), BF),
            pltpu.VMEM((CH, CH), BF),
            pltpu.VMEM((TAPS * PAIR, COUT), BF),
            pltpu.VMEM((CH, CH), BF),
            pltpu.VMEM((CH, PAIR), F32),
            pltpu.VMEM((2, TOKENS, PAIR), BF),
            pltpu.VMEM((2, TOKENS, PAIR), BF),
            pltpu.VMEM((PAIR, TOKENS), BF),
            pltpu.VMEM((PAIR, TOKENS), BF),
            pltpu.VMEM((2, TOKENS, TOKENS), F32),
            pltpu.VMEM((PAIR, TOKENS), BF),
            pltpu.VMEM((TOKENS, PAIR), BF),
            pltpu.VMEM((PAIR, CH), BF),
            pltpu.VMEM((TOKENS + 2 * GRID, TAPS * PAIR), F32),
            pltpu.VMEM((TOKENS, CH), BF),
            pltpu.VMEM((CH, PAIR), BF),
            pltpu.VMEM((OWN, 2 * TOKENS), BF),
            pltpu.VMEM((10 * OWN, 2 * TOKENS), BF),
            pltpu.VMEM((DP, ROWS, COUT), BF),
            pltpu.VMEM((DP, ROWS, COUT), BF),
            pltpu.VMEM((TOKENS, PAIR), BF),
            pltpu.VMEM((TOKENS, PAIR), F32),
            pltpu.VMEM((TOKENS, PAIR), F32),
            pltpu.VMEM((3, TOKENS, PAIR), BF),
            pltpu.VMEM((PAIR, CH), F32),
            pltpu.VMEM((SPACE, 2 * SLAB, CH // 2), BF),
            pltpu.VMEM((SPACE, 2 * SLAB, CH // 2), BF),
            pltpu.VMEM((SLAB, CH), F32),
            pltpu.VMEM((SLAB, CH), F32),
            sems((6,)),
            sems((SPACE,)), sems((SPACE,)),
            sems((SPACE,)), sems((SPACE,)),
            sems((CHIPS,)), sems((CHIPS,)),
            sems((CHIPS,)), sems((CHIPS,)),
            sems((SPACE,)), sems((SPACE,)),
            sems((DP,)), sems((DP,)),
            sems((SPACE,)), sems((SPACE,)),
            sems((SPACE,)), sems((SPACE,)),
            sems((2,)), sems((2,)),
        ],
        compiler_params=pltpu.CompilerParams(
            collective_id=0, has_side_effects=True, vmem_limit_bytes=58 * 1024 * 1024
        ),
        cost_estimate=pl.CostEstimate(
            flops=8_000_000_000, bytes_accessed=20_000_000, transcendentals=2_000_000
        ),
    )(queries, keys, values, cotangent, out_weight, wconv, bias)
    return grads[0], grads[1], grads[2], gw, jnp.transpose(gc, (1, 0, 2))


def solution(mesh):
    return jax.shard_map(
        on_device,
        mesh=mesh,
        in_specs=(
            P("dp", "space", None),
            P("dp", "space", None),
            P("dp", "space", None),
            P("dp", "space", None),
            P("dp"),
            P(),
            P(),
            P(),
        ),
        out_specs=(
            P("dp", "space", None),
            P("dp", "space", None),
            P("dp", "space", None),
            P(("dp", "space"), None),
            P(("dp", "space"), None, None),
        ),
        check_vma=False,
    )
```

```python
import jax
import jax.numpy as jnp
from jax import lax
from jax.experimental import pallas as pl
from jax.experimental.pallas import tpu as pltpu
from jax.sharding import PartitionSpec as P

HEAD_DIM = 64
TAPS = 9
GRID = 32
TOKENS = GRID * GRID
PAIR = 2 * HEAD_DIM
DP = 8
SPACE = 16
CHIPS = 8
CH = 1024
COUT = 640
HERE = 64
SLAB = 8
OWN = DP * SLAB
ROWS = 80
BLOCK = 256
SPLIT = 2
STEPS = 1000
SCALE = HEAD_DIM ** (-0.5)
MESH = pl.DeviceIdType.MESH
NT = (((1,), (1,)), ((), ()))
BF = jnp.bfloat16
F32 = jnp.float32


def mm(a, b):
    return jnp.dot(a, b, preferred_element_type=F32)


def mm_nt(a, b):
    return lax.dot_general(a, b, NT, preferred_element_type=F32)


def kernel(
    q_ref, k_ref, v_ref, cot_ref, w_ref, wc_ref, table_ref, step_ref,
    grads_ref, gw_ref, gc_ref,
    qkv, cot_all, cext, w, wc, table, wperm, bias_col, km, dom, vt, kt, probs, ot, att, att_tok,
    hg_tok, ag_tok, hsend, hbuf, lhs, conv_acc, conv_send, conv_recv, conv_keep, conv_out, conv_in, do, dv_acc, dk_acc, gh,
    ow_lhs, ow_pass, ow_in, ow_send, ow_recv, ow_keep, ow_out, ow_back, ow_sum, ow_parts,
    loc, halo_s, halo_r, qkv_s, qkv_r, near_s, near_r, cot_s, cot_r, ag_s, ag_r, att_s, att_r, hid_s, hid_r,
    conv_s, conv_r, cy_s, cy_r, ow_s, ow_r, oy_s, oy_r, sum_s, sum_r, gr_s, gr_r, one_s, one_r,
):
    d = lax.axis_index("dp")
    s = lax.axis_index("space")
    c = lax.div(s, 2)
    k = lax.rem(s, 2)
    lin = d * 2 + k
    z = lax.div(c, 2)
    column_y = lax.rem(c, 2)
    across = lax.div(d, 4)
    along = lax.rem(d, 4)
    partner = {"space": c * 2 + 1 - k}

    def lanes(chip):
        return pl.ds(pl.multiple_of(chip * PAIR, PAIR), PAIR)

    def rows(index, size):
        return pl.ds(pl.multiple_of(index * size, size), size)

    def to(i):
        return lax.rem(s + i, SPACE)

    def frm(i):
        return lax.rem(s + SPACE - i, SPACE)

    def chip_to(i):
        return lax.rem(c + i, CHIPS)

    def chip_frm(i):
        return lax.rem(c + CHIPS - i, CHIPS)

    def each(count, body):
        def step(i, carry):
            body(i)
            return carry

        lax.fori_loop(1, count, step, 0)

    def take(ref, sem):
        pltpu.make_async_copy(ref, ref, sem).wait()

    def remote(src, dst, send, recv, where):
        return pltpu.make_async_remote_copy(
            src_ref=src, dst_ref=dst, send_sem=send, recv_sem=recv,
            device_id=where, device_id_type=MESH,
        )

    local = [
        pltpu.make_async_copy(w_ref, w, loc.at[0]),
        pltpu.make_async_copy(cot_ref.at[k], cext.at[pl.ds(pl.multiple_of(GRID + k * HERE, GRID), HERE)], loc.at[1]),
        pltpu.make_async_copy(cot_ref.at[k], cot_all.at[rows(k * SPACE + s, HERE)], loc.at[2]),
        pltpu.make_async_copy(q_ref.at[k, :, lanes(c)], qkv.at[0, rows(s, HERE)], loc.at[3]),
        pltpu.make_async_copy(k_ref.at[k, :, lanes(c)], qkv.at[1, rows(s, HERE)], loc.at[4]),
        pltpu.make_async_copy(v_ref.at[k, :, lanes(c)], qkv.at[2, rows(s, HERE)], loc.at[5]),
        pltpu.make_async_copy(table_ref, table, loc.at[6]),
        pltpu.make_async_copy(wc_ref, wc, loc.at[7]),
    ]
    for copy in local:
        copy.start()

    barrier = pltpu.get_barrier_semaphore()

    def greet(i):
        pl.semaphore_signal(barrier, inc=1, device_id={"space": to(i)}, device_id_type=MESH)
        other = lax.rem(lin + i, SPACE)
        pl.semaphore_signal(
            barrier, inc=1,
            device_id={"dp": lax.div(other, 2), "space": c * 2 + lax.rem(other, 2)},
            device_id_type=MESH,
        )

    each(SPACE, greet)
    pl.semaphore_wait(barrier, 2 * (SPACE - 1))

    halo = remote(
        cot_ref.at[1 - k], cext.at[pl.ds(pl.multiple_of(GRID + k * HERE, GRID), HERE)],
        halo_s.at[0], halo_r.at[0], partner,
    )
    halo.start()
    low_end = pl.ds(0, GRID)
    high_end = pl.ds(GRID + PAIR, GRID)

    def edge(core, begin, place, slot, chip):
        return remote(
            cot_ref.at[core, pl.ds(begin, GRID)], cext.at[place],
            halo_s.at[1 + core], halo_r.at[slot], {"space": chip * 2 + core},
        )

    @pl.when((k == 1) & (c < CHIPS - 1))
    def _():
        for core in range(2):
            edge(core, GRID, low_end, 1, c + 1).start()

    @pl.when((k == 0) & (c > 0))
    def _():
        for core in range(2):
            edge(core, 0, high_end, 2, c - 1).start()

    @pl.when(c == 0)
    def _():
        cext[low_end] = jnp.zeros((GRID, COUT), BF)

    @pl.when(c == CHIPS - 1)
    def _():
        cext[high_end] = jnp.zeros((GRID, COUT), BF)

    def send_qkv(i):
        peer = to(i)
        chip = lax.div(peer, 2)
        core = lax.rem(peer, 2)
        for j, ref in enumerate((q_ref, k_ref, v_ref)):
            remote(
                ref.at[core, :, lanes(chip)], qkv.at[j, rows(s, HERE)],
                qkv_s.at[i], qkv_r.at[i], {"space": peer},
            ).start()

    each(SPACE, send_qkv)

    def near(core, step):
        chip = z * 2 + lax.rem(column_y + step, 2)
        return remote(
            cot_ref.at[core], cot_all.at[rows(core * SPACE + s, HERE)],
            near_s.at[core, step], near_r.at[k, step], {"space": chip * 2 + core},
        )

    for core in range(2):
        near(core, 1).start()

        @pl.when(core != k)
        def _():
            near(core, 0).start()

    local[0].wait()
    local[6].wait()
    bias_here = table[pl.ds(step_ref[k], 1), :]
    high = bias_here.astype(BF)
    rest = bias_here - high.astype(F32)
    mid = rest.astype(BF)
    low = (rest - mid.astype(F32)).astype(BF)
    pieces = jnp.concatenate(
        [high.astype(F32), mid.astype(F32), low.astype(F32), jnp.zeros((13, CH), F32)], axis=0
    ).astype(BF)

    def permute(i, carry):
        n = lax.broadcasted_iota(jnp.int32, (BLOCK, CH), 0) + i * BLOCK
        e = lax.broadcasted_iota(jnp.int32, (BLOCK, CH), 1)
        n_chip = lax.shift_right_logical(n, 7)
        n_core = lax.shift_right_logical(n, 6) & 1
        n_dp = lax.shift_right_logical(n, 3) & 7
        target = n_dp * 128 + n_chip * 16 + n_core * 8 + (n & 7)
        pick = jnp.where(e == target, 1.0, 0.0).astype(BF)
        wperm[rows(i, BLOCK), :] = mm_nt(pick, w[...]).astype(BF)
        column = jnp.sum(mm_nt(pick, pieces), axis=1, keepdims=True)
        bias_col[rows(i, BLOCK), :] = jnp.broadcast_to(column, (BLOCK, PAIR))
        return carry

    lax.fori_loop(0, CH // BLOCK, permute, 0)

    local[1].wait()
    local[7].wait()
    halo.wait_send()
    take(cext.at[pl.ds(0, HERE)], halo_r.at[0])

    @pl.when(c > 0)
    def _():
        take(cext.at[low_end], halo_r.at[1])

    @pl.when(c < CHIPS - 1)
    def _():
        take(cext.at[high_end], halo_r.at[2])

    sums = []
    for col in range(3):
        total = None
        for row in range(3):
            start = 2 * GRID - GRID * row
            part = mm_nt(cext[start : start + PAIR, :], wc[3 * row + col])
            total = part if total is None else total + part
        sums.append(total)
    column = lax.broadcasted_iota(jnp.int32, (PAIR, CH), 0) & (GRID - 1)
    hidden_grad = (
        sums[1]
        + jnp.where(column < GRID - 1, pltpu.roll(sums[0], PAIR - 1, 0), 0.0)
        + jnp.where(column > 0, pltpu.roll(sums[2], 1, 0), 0.0)
    )
    hg_tok[...] = hidden_grad.astype(BF)
    ag_tok[...] = mm_nt(hg_tok[...], w[...]).astype(BF)

    def send_ag(i):
        chip = chip_to(i)
        remote(
            ag_tok.at[:, lanes(chip)], do.at[rows(c, PAIR)],
            ag_s.at[i], ag_r.at[i], {"space": chip * 2 + k},
        ).start()

    each(CHIPS, send_ag)
    do[rows(c, PAIR), :] = ag_tok[:, lanes(c)]

    for copy in local[3:6]:
        copy.wait()
    each(SPACE, lambda i: take(qkv.at[:, rows(frm(i), HERE), :], qkv_r.at[i]))

    def quarter(zz):
        return cot_all.at[pl.ds(pl.multiple_of(k * TOKENS + zz * 2 * PAIR, PAIR), 2 * PAIR)]

    def eighth(zz, part):
        begin = k * TOKENS + zz * 2 * PAIR + part * PAIR
        return cot_all.at[pl.ds(pl.multiple_of(begin, PAIR), PAIR)]

    z_up = lax.rem(z + 1, 4)
    z_down = lax.rem(z + 3, 4)
    up = {"space": (z_up * 2 + column_y) * 2 + k}
    down = {"space": (z_down * 2 + column_y) * 2 + k}
    small = cot_all.at[pl.ds(0, HERE)]
    local[2].wait()
    take(small, near_r.at[1 - k, 0])
    take(small, near_r.at[0, 1])
    take(small, near_r.at[1, 1])
    ring = [
        remote(quarter(z), quarter(z), cot_s.at[0], cot_r.at[0], up),
        remote(quarter(z), quarter(z), cot_s.at[1], cot_r.at[1], down),
        remote(eighth(z_down, 0), eighth(z_down, 0), cot_s.at[2], cot_r.at[2], up),
        remote(eighth(z_up, 1), eighth(z_up, 1), cot_s.at[3], cot_r.at[3], down),
    ]
    ring[0].start()
    ring[1].start()
    first = lax.broadcasted_iota(jnp.int32, (TOKENS, PAIR), 1) < HEAD_DIM
    key = qkv[1]
    km[0] = jnp.where(first, key, jnp.zeros_like(key))
    km[1] = jnp.where(first, jnp.zeros_like(key), key)
    kt[...] = key.astype(F32).T.astype(BF)
    vt[...] = qkv[2].astype(F32).T.astype(BF)

    def forward(i, carry):
        here = rows(i, BLOCK)
        query = qkv[0, here, :] * jnp.asarray(SCALE, BF)
        outs = []
        for h in range(2):
            scores = mm_nt(km[h], query)
            top = jnp.max(scores, axis=0, keepdims=True)
            shifted = jnp.exp(scores - top)
            total = jnp.sum(shifted, axis=0, keepdims=True)
            prob = shifted * (1.0 / total)
            probs[h, :, here] = prob
            outs.append(mm(vt[h * HEAD_DIM : (h + 1) * HEAD_DIM, :], prob.astype(BF)))
        out = jnp.concatenate(outs, axis=0)
        ot[:, here] = out.astype(BF)
        att[here, :] = out.T.astype(BF)
        for half in range(2):
            chip = 2 * i + half

            @pl.when(chip != c)
            def _():
                remote(
                    att.at[rows(chip, PAIR)], att_tok.at[:, lanes(c)],
                    att_s.at[chip], att_r.at[c], {"space": chip * 2 + k},
                ).start()

        return carry

    lax.fori_loop(0, TOKENS // BLOCK, forward, 0)
    att_tok[:, lanes(c)] = att[rows(c, PAIR), :]

    each(CHIPS, lambda i: take(do.at[rows(chip_frm(i), PAIR)], ag_r.at[i]))
    grad = do[...]
    dom[0] = jnp.where(first, grad, jnp.zeros_like(grad))
    dom[1] = jnp.where(first, jnp.zeros_like(grad), grad)
    dv_acc[...] = jnp.zeros_like(dv_acc)
    dk_acc[...] = jnp.zeros_like(dk_acc)

    def backward(i, carry):
        here = rows(i, BLOCK)
        query = qkv[0, here, :] * jnp.asarray(SCALE, BF)
        half = lax.broadcasted_iota(jnp.int32, (BLOCK, PAIR), 1) < HEAD_DIM
        product = ot[:, here].astype(F32) * do[here, :].astype(F32).T
        outs = []
        for h in range(2):
            prob = probs[h, :, here]
            grad_block = dom[h, here, :]
            dv_acc[...] += mm(prob.astype(BF), grad_block)
            prob_grad = mm_nt(qkv[2], grad_block)
            delta = jnp.sum(product[h * HEAD_DIM : (h + 1) * HEAD_DIM], axis=0, keepdims=True)
            score_grad = (prob * (prob_grad - delta)).astype(BF)
            zero = jnp.zeros_like(query)
            masked = jnp.where(half, query, zero) if h == 0 else jnp.where(half, zero, query)
            dk_acc[...] += mm(score_grad, masked)
            outs.append(mm(kt[h * HEAD_DIM : (h + 1) * HEAD_DIM, :], score_grad))
        gh[0, here, :] = (jnp.concatenate(outs, axis=0) * SCALE).T.astype(BF)
        return carry

    lax.fori_loop(0, SPLIT, backward, 0)

    take(quarter(z_down), cot_r.at[0])
    ring[2].start()
    take(quarter(z_up), cot_r.at[1])
    ring[3].start()

    each(CHIPS, lambda i: take(att_tok.at[:, lanes(chip_frm(i))], att_r.at[chip_frm(i)]))
    hsend[...] = (mm_nt(wperm[...], att_tok[...]) + bias_col[...]).astype(BF)

    def send_hidden(i):
        peer = to(i)
        remote(
            hsend.at[rows(peer, OWN)], hbuf.at[:, lanes(k * CHIPS + c)],
            hid_s.at[i], hid_r.at[i], {"space": peer},
        ).start()

    each(SPACE, send_hidden)
    hbuf[:, lanes(k * CHIPS + c)] = hsend[rows(s, OWN), :]

    flipped = att_tok[...].astype(F32).T.reshape(DP, CHIPS, 2, SLAB, PAIR)
    for core in range(2):
        for xx in range(4):
            for yy in range(2):
                at = (xx * 2 + yy) * HERE
                rows_of = flipped[yy * 4 + xx, :, core].reshape(HERE, PAIR)
                ow_lhs[core, at : at + HERE, :] = rows_of.astype(BF)

    def pass_on(i, carry):
        ow_pass[rows(i, PAIR), :] = mm(ow_lhs[1 - k, rows(i, PAIR), :], hg_tok[...]).astype(BF)
        return carry

    lax.fori_loop(0, 4, pass_on, 0)
    ow_copy = remote(ow_pass, ow_in, one_s.at[1], one_r.at[1], partner)
    ow_copy.start()

    lax.fori_loop(SPLIT, TOKENS // BLOCK, backward, 0)
    gh[1] = dk_acc[...].astype(BF)
    gh[2] = dv_acc[...].astype(BF)

    ow_copy.wait()

    def join(i, carry):
        both = mm(ow_lhs[k, rows(i, PAIR), :], hg_tok[...]) + ow_in[rows(i, PAIR), :].astype(F32)
        ow_send[rows(i, PAIR), :] = both.astype(BF)
        return carry

    lax.fori_loop(0, 4, join, 0)

    def send_ow(i):
        dest = lax.rem(along + i, 4)
        remote(
            ow_send.at[rows(dest, PAIR)], ow_recv.at[i], ow_s.at[i], ow_r.at[i],
            {"dp": across * 4 + dest},
        ).start()

    each(4, send_ow)

    z_far = lax.rem(z + 2, 4)
    take(eighth(z_far, 0), cot_r.at[2])
    take(eighth(z_far, 1), cot_r.at[3])
    mine = rows(k, TOKENS)
    cot_copy = remote(cot_all.at[mine], cot_all.at[mine], one_s.at[0], one_r.at[0], partner)
    cot_copy.start()

    def send_grads(i):
        peer = to(i)
        remote(
            gh.at[:, rows(peer, HERE), :], grads_ref.at[:, k, :, lanes(c)],
            gr_s.at[i], gr_r.at[i], {"space": peer},
        ).start()

    each(SPACE, send_grads)
    own_grads = pltpu.make_async_copy(
        gh.at[:, rows(s, HERE), :], grads_ref.at[:, k, :, lanes(c)], loc.at[0]
    )
    own_grads.start()

    def take_hidden(i):
        peer = frm(i)
        take(hbuf.at[:, lanes(lax.rem(peer, 2) * CHIPS + lax.div(peer, 2))], hid_r.at[i])

    each(SPACE, take_hidden)

    spot = lax.broadcasted_iota(jnp.int32, (OWN, TOKENS), 1)
    y = lax.shift_right_logical(spot, 5)
    x = spot & (GRID - 1)
    for sample in range(2):
        hidden = hbuf[:, sample * TOKENS : (sample + 1) * TOKENS].astype(F32)
        for row in range(3):
            for col in range(3):
                offset = (row - 1) * GRID + col - 1
                moved = pltpu.roll(hidden, (-offset) % TOKENS, 1) if offset else hidden
                good = None
                for ok in (
                    [y > 0] * (row == 0) + [y < GRID - 1] * (row == 2)
                    + [x > 0] * (col == 0) + [x < GRID - 1] * (col == 2)
                ):
                    good = ok if good is None else good & ok
                if good is not None:
                    moved = jnp.where(good, moved, 0.0)
                tap = 3 * row + col
                lhs[sample, tap * OWN : (tap + 1) * OWN, :] = moved.astype(BF)
        lhs[sample, TAPS * OWN :, :] = jnp.zeros((OWN, TOKENS), BF)
    tiles = [(at, min(at + BLOCK, COUT)) for at in range(0, COUT, BLOCK)]
    for at, end in tiles:
        conv_acc[:, at:end] = mm(lhs[k], cot_all[mine, at:end])
    cot_copy.wait_send()
    other = rows(1 - k, TOKENS)
    take(cot_all.at[other], one_r.at[0])
    for tile, (at, end) in enumerate(tiles):
        part = conv_acc[:, at:end] + mm(lhs[1 - k], cot_all[other, at:end])
        for dest in range(DP):
            for pair in range(5):
                top = pair * 2 * OWN + dest * SLAB
                both = jnp.concatenate(
                    [part[top : top + SLAB], part[top + OWN : top + OWN + SLAB]], axis=0
                )
                conv_send[dest % 4, dest // 4, pair * 16 : pair * 16 + 16, at:end] = both.astype(BF)

        def send_conv(i):
            dest = lax.rem(along + i, 4)
            remote(
                conv_send.at[dest, :, :, at:end], conv_recv.at[i, :, :, at:end],
                conv_s.at[tile, i], conv_r.at[tile, i], {"dp": across * 4 + dest},
            ).start()

        each(4, send_conv)

    opposite = {"dp": lax.rem(d + 4, DP)}
    each(4, lambda i: take(ow_recv.at[i], ow_r.at[i]))
    total = ow_send[rows(along, PAIR), :].astype(F32)
    for i in range(1, 4):
        total = total + ow_recv[i].astype(F32)
    ow_keep[...] = total
    ow_out[...] = ow_keep[rows(1 - across, HERE), :].astype(BF)
    ow_turn = remote(ow_out, ow_back, oy_s.at[0], oy_r.at[0], opposite)
    ow_turn.start()

    turns = []
    for tile, (at, end) in enumerate(tiles):
        each(4, lambda i: take(conv_recv.at[i, :, :, at:end], conv_r.at[tile, i]))
        for half in range(2):
            total = conv_send[along, half, :, at:end].astype(F32)
            for i in range(1, 4):
                total = total + conv_recv[i, half, :, at:end].astype(F32)
            conv_keep[half, :, at:end] = total
        conv_out[:, at:end] = conv_keep[1 - across, :, at:end].astype(BF)
        turn = remote(
            conv_out.at[:, at:end], conv_in.at[:, at:end], cy_s.at[tile], cy_r.at[tile], opposite
        )
        turn.start()
        turns.append(turn)

    ow_turn.wait()
    ow_sum[...] = ow_keep[rows(across, HERE), :] + ow_back[...].astype(F32)

    def send_sum(i):
        chip = chip_to(i)
        remote(
            ow_sum.at[rows(chip, SLAB)], ow_parts.at[i],
            sum_s.at[i], sum_r.at[i], {"space": chip * 2 + k},
        ).start()

    each(CHIPS, send_sum)

    for tile, (at, end) in enumerate(tiles):
        turns[tile].wait()
        total = conv_keep[across, :, at:end] + conv_in[:, at:end].astype(F32)
        for tap in range(TAPS):
            gc_ref[tap, :, at:end] = total[tap * SLAB : (tap + 1) * SLAB]

    each(CHIPS, lambda i: take(ow_parts.at[i], sum_r.at[i]))
    total = ow_sum[rows(c, SLAB), :]
    for i in range(1, CHIPS):
        total = total + ow_parts[i]
    gw_ref[...] = total

    own_grads.wait()

    def take_grads(i):
        peer = frm(i)
        take(grads_ref.at[:, lax.rem(peer, 2), :, lanes(lax.div(peer, 2))], gr_r.at[i])

    each(SPACE, take_grads)

    def sent(i):
        take(qkv.at[:, rows(0, HERE), :], qkv_s.at[i])
        take(hsend.at[rows(0, OWN)], hid_s.at[i])
        take(gh.at[:, rows(0, HERE), :], gr_s.at[i])

    each(SPACE, sent)

    def sent_chips(i):
        take(att.at[rows(0, PAIR)], att_s.at[chip_to(i)])
        take(ag_tok.at[:, lanes(0)], ag_s.at[i])
        take(ow_sum.at[rows(0, SLAB)], sum_s.at[i])

    each(CHIPS, sent_chips)

    def sent_along(i):
        take(ow_send.at[rows(0, PAIR)], ow_s.at[i])
        for tile, (at, end) in enumerate(tiles):
            take(conv_send.at[0, :, :, at:end], conv_s.at[tile, i])

    each(4, sent_along)
    for copy in ring:
        copy.wait_send()
    for core in range(2):
        take(small, near_s.at[core, 1])
    take(small, near_s.at[1 - k, 0])

    @pl.when(((k == 1) & (c < CHIPS - 1)) | ((k == 0) & (c > 0)))
    def _():
        for core in range(2):
            take(cext.at[low_end], halo_s.at[1 + core])


def hand_over(*refs):
    sources, outs, held, sems = refs[:3], refs[3:8], refs[8:13], refs[13]
    grads_ref, gw_ref, gc_ref = sources
    ins = [grads_ref.at[0], grads_ref.at[1], grads_ref.at[2], gw_ref, gc_ref]
    arrive = [pltpu.make_async_copy(a, b, sems.at[0, j]) for j, (a, b) in enumerate(zip(ins, held))]
    leave = [pltpu.make_async_copy(a, b, sems.at[1, j]) for j, (a, b) in enumerate(zip(held, outs))]
    for copy in arrive:
        copy.start()
    for first, second in zip(arrive, leave):
        first.wait()
        second.start()
    for copy in leave:
        copy.wait()


def on_device(queries, keys, values, cotangent, timesteps, time_table, out_weight, conv_weight):
    anywhere = pl.BlockSpec(memory_space=pl.ANY)
    vmem = pl.BlockSpec(memory_space=pltpu.VMEM)
    sems = pltpu.SemaphoreType.DMA
    wide = jax.ShapeDtypeStruct((2, HERE, CH), BF)
    gw_shape = jax.ShapeDtypeStruct((SLAB, CH), F32)
    gc_shape = jax.ShapeDtypeStruct((TAPS, SLAB, COUT), F32)
    parts = pl.pallas_call(
        kernel,
        out_shape=(jax.ShapeDtypeStruct((3, 2, HERE, CH), BF), gw_shape, gc_shape),
        in_specs=[anywhere] * 7 + [pl.BlockSpec(memory_space=pltpu.SMEM)],
        out_specs=(anywhere, vmem, vmem),
        scratch_shapes=[
            pltpu.VMEM((3, TOKENS, PAIR), BF),
            pltpu.VMEM((2 * TOKENS, COUT), BF),
            pltpu.VMEM((PAIR + 2 * GRID, COUT), BF),
            pltpu.VMEM((CH, CH), BF),
            pltpu.VMEM((TAPS, CH, COUT), BF),
            pltpu.VMEM((STEPS, CH), F32),
            pltpu.VMEM((CH, CH), BF),
            pltpu.VMEM((CH, PAIR), F32),
            pltpu.VMEM((2, TOKENS, PAIR), BF),
            pltpu.VMEM((2, TOKENS, PAIR), BF),
            pltpu.VMEM((PAIR, TOKENS), BF),
            pltpu.VMEM((PAIR, TOKENS), BF),
            pltpu.VMEM((2, TOKENS, TOKENS), F32),
            pltpu.VMEM((PAIR, TOKENS), BF),
            pltpu.VMEM((TOKENS, PAIR), BF),
            pltpu.VMEM((PAIR, CH), BF),
            pltpu.VMEM((PAIR, CH), BF),
            pltpu.VMEM((PAIR, CH), BF),
            pltpu.VMEM((CH, PAIR), BF),
            pltpu.VMEM((OWN, 2 * TOKENS), BF),
            pltpu.VMEM((2, 10 * OWN, TOKENS), BF),
            pltpu.VMEM((10 * OWN, COUT), F32),
            pltpu.VMEM((4, 2, ROWS, COUT), BF),
            pltpu.VMEM((4, 2, ROWS, COUT), BF),
            pltpu.VMEM((2, ROWS, COUT), F32),
            pltpu.VMEM((ROWS, COUT), BF),
            pltpu.VMEM((ROWS, COUT), BF),
            pltpu.VMEM((TOKENS, PAIR), BF),
            pltpu.VMEM((TOKENS, PAIR), F32),
            pltpu.VMEM((TOKENS, PAIR), F32),
            pltpu.VMEM((3, TOKENS, PAIR), BF),
            pltpu.VMEM((2, CH // 2, PAIR), BF),
            pltpu.VMEM((CH // 2, CH), BF),
            pltpu.VMEM((CH // 2, CH), BF),
            pltpu.VMEM((CH // 2, CH), BF),
            pltpu.VMEM((4, PAIR, CH), BF),
            pltpu.VMEM((PAIR, CH), F32),
            pltpu.VMEM((HERE, CH), BF),
            pltpu.VMEM((HERE, CH), BF),
            pltpu.VMEM((HERE, CH), F32),
            pltpu.VMEM((CHIPS, SLAB, CH), F32),
            sems((8,)),
            sems((3,)), sems((3,)),
            sems((SPACE,)), sems((SPACE,)),
            sems((2, 2)), sems((2, 2)),
            sems((4,)), sems((4,)),
            sems((CHIPS,)), sems((CHIPS,)),
            sems((CHIPS,)), sems((CHIPS,)),
            sems((SPACE,)), sems((SPACE,)),
            sems((3, 4)), sems((3, 4)),
            sems((3,)), sems((3,)),
            sems((4,)), sems((4,)),
            sems((1,)), sems((1,)),
            sems((CHIPS,)), sems((CHIPS,)),
            sems((SPACE,)), sems((SPACE,)),
            sems((2,)), sems((2,)),
        ],
        compiler_params=pltpu.CompilerParams(
            collective_id=0, has_side_effects=True, vmem_limit_bytes=60 * 1024 * 1024
        ),
        cost_estimate=pl.CostEstimate(
            flops=8_000_000_000, bytes_accessed=20_000_000, transcendentals=2_000_000
        ),
    )(
        queries, keys, values, cotangent, out_weight, jnp.transpose(conv_weight, (1, 0, 2)),
        time_table, timesteps,
    )
    gq, gk, gv, gw, gc = pl.pallas_call(
        hand_over,
        out_shape=(wide, wide, wide, gw_shape, gc_shape),
        in_specs=[anywhere] * 3,
        out_specs=(anywhere,) * 5,
        scratch_shapes=[pltpu.VMEM((2, HERE, CH), BF)] * 3
        + [pltpu.VMEM((SLAB, CH), F32), pltpu.VMEM((TAPS, SLAB, COUT), F32), sems((2, 5))],
    )(*parts)
    return gq, gk, gv, gw, jnp.transpose(gc, (1, 0, 2))


def solution(mesh):
    return jax.shard_map(
        on_device,
        mesh=mesh,
        in_specs=(
            P("dp", "space", None),
            P("dp", "space", None),
            P("dp", "space", None),
            P("dp", "space", None),
            P("dp"),
            P(),
            P(),
            P(),
        ),
        out_specs=(
            P("dp", "space", None),
            P("dp", "space", None),
            P("dp", "space", None),
            P(("dp", "space"), None),
            P(("dp", "space"), None, None),
        ),
        check_vma=False,
    )
```

```python
import jax
import jax.numpy as jnp
from jax import lax
from jax.experimental import pallas as pl
from jax.experimental.pallas import tpu as pltpu
from jax.sharding import PartitionSpec as P

HEAD_DIM = 64
TAPS = 9
GRID = 32
TOKENS = GRID * GRID
PAIR = 2 * HEAD_DIM
DP = 8
SPACE = 16
CHIPS = 8
CH = 1024
COUT = 640
HERE = 64
SLAB = 8
OWN = DP * SLAB
ROWS = 80
BLOCK = 256
STEPS = 1000
HALF = CH // 2
SCALE = HEAD_DIM ** (-0.5)
MESH = pl.DeviceIdType.MESH
NT = (((1,), (1,)), ((), ()))
BF = jnp.bfloat16
F32 = jnp.float32


def mm(a, b):
    return jnp.dot(a, b, preferred_element_type=F32)


def mm_nt(a, b):
    return lax.dot_general(a, b, NT, preferred_element_type=F32)


def kernel(
    q_ref, k_ref, v_ref, cot_ref, w_ref, wc_ref, table_ref, step_ref,
    grads_ref, gw_ref, gc_ref,
    qkv, cot_all, cext, w, wc, table, wperm, bias_col, qm, dom, vt, kt, probs, ot, att, att_tok,
    hg_tok, ag_tok, hsend, hbuf, lhs, conv_acc, conv_send, conv_recv, conv_keep, conv_out, conv_in, do, delta, dq_acc, gh,
    ow_lhs, ow_pass, ow_in, ow_send, ow_recv, ow_keep, ow_x, ow_xr, ow_y, ow_parts,
    loc, halo_s, halo_r, qkv_s, qkv_r, near_s, near_r, cot_s, cot_r, hop_s, hop_r, share_s, share_r, ag_s, ag_r, att_s, att_r, hid_s, hid_r,
    conv_s, conv_r, cy_s, cy_r, ow_s, ow_r, ox_s, ox_r, oy_s, oy_r, gr_s, gr_r, gq_s, gq_r, one_s, one_r,
):
    d = lax.axis_index("dp")
    s = lax.axis_index("space")
    c = lax.div(s, 2)
    k = lax.rem(s, 2)
    lin = d * 2 + k
    z = lax.div(c, 2)
    column_y = lax.rem(c, 2)
    across = lax.div(d, 4)
    along = lax.rem(d, 4)
    partner = {"space": c * 2 + 1 - k}

    def lanes(chip):
        return pl.ds(pl.multiple_of(chip * PAIR, PAIR), PAIR)

    def rows(index, size):
        return pl.ds(pl.multiple_of(index * size, size), size)

    def to(i):
        return lax.rem(s + i, SPACE)

    def frm(i):
        return lax.rem(s + SPACE - i, SPACE)

    def chip_to(i):
        return lax.rem(c + i, CHIPS)

    def chip_frm(i):
        return lax.rem(c + CHIPS - i, CHIPS)

    def each(count, body):
        def step(i, carry):
            body(i)
            return carry

        lax.fori_loop(1, count, step, 0)

    def take(ref, sem):
        pltpu.make_async_copy(ref, ref, sem).wait()

    def remote(src, dst, send, recv, where):
        return pltpu.make_async_remote_copy(
            src_ref=src, dst_ref=dst, send_sem=send, recv_sem=recv,
            device_id=where, device_id_type=MESH,
        )

    local = [
        pltpu.make_async_copy(w_ref, w, loc.at[0]),
        pltpu.make_async_copy(cot_ref.at[k], cext.at[pl.ds(pl.multiple_of(GRID + k * HERE, GRID), HERE)], loc.at[1]),
        pltpu.make_async_copy(cot_ref.at[k], cot_all.at[rows(k * SPACE + s, HERE)], loc.at[2]),
        pltpu.make_async_copy(q_ref.at[k, :, lanes(c)], qkv.at[0, rows(s, HERE)], loc.at[3]),
        pltpu.make_async_copy(k_ref.at[k, :, lanes(c)], qkv.at[1, rows(s, HERE)], loc.at[4]),
        pltpu.make_async_copy(v_ref.at[k, :, lanes(c)], qkv.at[2, rows(s, HERE)], loc.at[5]),
        pltpu.make_async_copy(table_ref, table, loc.at[6]),
        pltpu.make_async_copy(wc_ref, wc, loc.at[7]),
    ]
    for copy in local:
        copy.start()

    barrier = pltpu.get_barrier_semaphore()

    def greet(i):
        pl.semaphore_signal(barrier, inc=1, device_id={"space": to(i)}, device_id_type=MESH)
        other = lax.rem(lin + i, SPACE)
        pl.semaphore_signal(
            barrier, inc=1,
            device_id={"dp": lax.div(other, 2), "space": c * 2 + lax.rem(other, 2)},
            device_id_type=MESH,
        )

    each(SPACE, greet)
    diagonal = {"dp": lax.rem(d + 4, DP), "space": (z * 2 + 1 - column_y) * 2 + k}
    pl.semaphore_signal(barrier, inc=1, device_id=diagonal, device_id_type=MESH)
    pl.semaphore_wait(barrier, 2 * (SPACE - 1) + 1)

    halo = remote(
        cot_ref.at[1 - k], cext.at[pl.ds(pl.multiple_of(GRID + k * HERE, GRID), HERE)],
        halo_s.at[0], halo_r.at[0], partner,
    )
    halo.start()
    low_end = pl.ds(0, GRID)
    high_end = pl.ds(GRID + PAIR, GRID)

    def edge(core, begin, place, slot, chip):
        return remote(
            cot_ref.at[core, pl.ds(begin, GRID)], cext.at[place],
            halo_s.at[1 + core], halo_r.at[slot], {"space": chip * 2 + core},
        )

    @pl.when((k == 1) & (c < CHIPS - 1))
    def _():
        for core in range(2):
            edge(core, GRID, low_end, 1, c + 1).start()

    @pl.when((k == 0) & (c > 0))
    def _():
        for core in range(2):
            edge(core, 0, high_end, 2, c - 1).start()

    @pl.when(c == 0)
    def _():
        cext[low_end] = jnp.zeros((GRID, COUT), BF)

    @pl.when(c == CHIPS - 1)
    def _():
        cext[high_end] = jnp.zeros((GRID, COUT), BF)

    def send_heads(i, arrays, sem):
        peer = to(i)
        chip = lax.div(peer, 2)
        core = lax.rem(peer, 2)
        for j, ref in arrays:
            remote(
                ref.at[core, :, lanes(chip)], qkv.at[j, rows(s, HERE)],
                qkv_s.at[sem], qkv_r.at[sem], {"space": peer},
            ).start()

    each(SPACE, lambda i: send_heads(i, ((0, q_ref), (1, k_ref)), 0))
    each(SPACE, lambda i: send_heads(i, ((2, v_ref),), 1))

    def near(core, step):
        chip = z * 2 + lax.rem(column_y + step, 2)
        return remote(
            cot_ref.at[core], cot_all.at[rows(core * SPACE + s, HERE)],
            near_s.at[core, step], near_r.at[k, step], {"space": chip * 2 + core},
        )

    for core in range(2):
        near(core, 1).start()

        @pl.when(core != k)
        def _():
            near(core, 0).start()

    for i, (shift_z, shift_y) in enumerate(((1, 0), (3, 0), (2, 0), (2, 1)), 1):
        chip = lax.rem(z + shift_z, 4) * 2 + lax.rem(column_y + shift_y, 2)
        for core in range(2):
            remote(
                cot_ref.at[core], cot_all.at[rows(core * SPACE + s, HERE)],
                cot_s.at[i, core], cot_r.at[i, k], {"space": chip * 2 + core},
            ).start()

    local[0].wait()
    local[6].wait()
    bias_here = table[pl.ds(step_ref[k], 1), :]
    high = bias_here.astype(BF)
    rest = bias_here - high.astype(F32)
    mid = rest.astype(BF)
    low = (rest - mid.astype(F32)).astype(BF)
    pieces = jnp.concatenate(
        [high.astype(F32), mid.astype(F32), low.astype(F32), jnp.zeros((13, CH), F32)], axis=0
    ).astype(BF)

    def permute(i, carry):
        n = lax.broadcasted_iota(jnp.int32, (BLOCK, CH), 0) + i * BLOCK
        e = lax.broadcasted_iota(jnp.int32, (BLOCK, CH), 1)
        n_chip = lax.shift_right_logical(n, 7)
        n_core = lax.shift_right_logical(n, 6) & 1
        n_dp = lax.shift_right_logical(n, 3) & 7
        target = n_dp * 128 + n_chip * 16 + n_core * 8 + (n & 7)
        pick = jnp.where(e == target, 1.0, 0.0).astype(BF)
        wperm[rows(i, BLOCK), :] = mm_nt(pick, w[...]).astype(BF)
        column = jnp.sum(mm_nt(pick, pieces), axis=1, keepdims=True)
        bias_col[rows(i, BLOCK), :] = jnp.broadcast_to(column, (BLOCK, PAIR))
        return carry

    lax.fori_loop(0, CH // BLOCK, permute, 0)

    local[1].wait()
    local[7].wait()
    halo.wait_send()
    take(cext.at[pl.ds(0, HERE)], halo_r.at[0])

    @pl.when(c > 0)
    def _():
        take(cext.at[low_end], halo_r.at[1])

    @pl.when(c < CHIPS - 1)
    def _():
        take(cext.at[high_end], halo_r.at[2])

    sums = []
    for col in range(3):
        total = None
        for row in range(3):
            start = 2 * GRID - GRID * row
            part = mm_nt(cext[start : start + PAIR, :], wc[3 * row + col])
            total = part if total is None else total + part
        sums.append(total)
    column = lax.broadcasted_iota(jnp.int32, (PAIR, CH), 0) & (GRID - 1)
    hidden_grad = (
        sums[1]
        + jnp.where(column < GRID - 1, pltpu.roll(sums[0], PAIR - 1, 0), 0.0)
        + jnp.where(column > 0, pltpu.roll(sums[2], 1, 0), 0.0)
    )
    hg_tok[...] = hidden_grad.astype(BF)
    ag_tok[...] = mm_nt(hg_tok[...], w[...]).astype(BF)

    def send_ag(i):
        chip = chip_to(i)
        remote(
            ag_tok.at[:, lanes(chip)], do.at[rows(c, PAIR)],
            ag_s.at[0], ag_r.at[0], {"space": chip * 2 + k},
        ).start()


    most = pl.ds(0, TOKENS - HERE)
    chips = pl.ds(0, TOKENS - PAIR)
    for copy in local[3:6]:
        copy.wait()
    take(qkv.at[pl.ds(0, 2), most], qkv_r.at[0])

    def block(zz, yy):
        return cot_all.at[pl.ds(pl.multiple_of(k * TOKENS + (zz * 2 + yy) * PAIR, PAIR), PAIR)]

    z_up = lax.rem(z + 1, 4)
    z_down = lax.rem(z + 3, 4)
    z_far = lax.rem(z + 2, 4)
    other_y = 1 - column_y
    small = cot_all.at[pl.ds(0, HERE)]
    ring = []
    for j, (zz, yy, chip) in enumerate((
        (z, other_y, z_up * 2 + column_y),
        (z, other_y, z_down * 2 + column_y),
    )):
        ring.append(
            remote(
                block(zz, yy), block(zz, yy), hop_s.at[j], hop_r.at[j], {"space": chip * 2 + k}
            )
        )
    own_blocks = ((z, 0), (z, 1), (z_up, column_y), (z_down, column_y), (z_far, 0), (z_far, 1))
    hop_blocks = ((z_down, other_y), (z_up, other_y))

    def share(blocks, slot):
        for zz, yy in blocks:
            remote(
                block(zz, yy), block(zz, yy), share_s.at[slot], share_r.at[slot], partner
            ).start()

    first = lax.broadcasted_iota(jnp.int32, (TOKENS, PAIR), 1) < HEAD_DIM
    query = qkv[0] * jnp.asarray(SCALE, BF)
    qm[0] = jnp.where(first, query, jnp.zeros_like(query))
    qm[1] = jnp.where(first, jnp.zeros_like(query), query)

    def weigh(i, carry):
        here = rows(i, BLOCK)
        for h in range(2):
            scores = mm_nt(qkv[1], qm[h, here, :])
            top = jnp.max(scores, axis=0, keepdims=True)
            shifted = jnp.exp(scores - top)
            total = jnp.sum(shifted, axis=0, keepdims=True)
            probs[h, :, here] = (shifted * (1.0 / total)).astype(BF)
        return carry

    lax.fori_loop(0, TOKENS // BLOCK, weigh, 0)
    local[2].wait()
    take(small, near_r.at[1 - k, 0])
    take(small, near_r.at[0, 1])
    take(small, near_r.at[1, 1])
    ring[0].start()
    ring[1].start()
    take(qkv.at[2, most], qkv_r.at[1])
    vt[...] = qkv[2].astype(F32).T.astype(BF)

    def forward(i, carry):
        here = rows(i, BLOCK)
        outs = [
            mm(vt[h * HEAD_DIM : (h + 1) * HEAD_DIM, :], probs[h, :, here]) for h in range(2)
        ]
        out = jnp.concatenate(outs, axis=0)
        ot[:, here] = out.astype(BF)
        att[here, :] = out.T.astype(BF)
        for half in range(2):
            chip = 2 * i + half

            @pl.when(chip != c)
            def _():
                remote(
                    att.at[rows(chip, PAIR)], att_tok.at[:, lanes(c)],
                    att_s.at[0], att_r.at[0], {"space": chip * 2 + k},
                ).start()

        return carry

    lax.fori_loop(0, TOKENS // BLOCK, forward, 0)
    att_tok[:, lanes(c)] = att[rows(c, PAIR), :]

    take(att.at[chips], att_r.at[0])
    hsend[...] = (mm_nt(wperm[...], att_tok[...]) + bias_col[...]).astype(BF)

    def send_hidden(i):
        peer = to(i)
        remote(
            hsend.at[rows(peer, OWN)], hbuf.at[:, lanes(k * CHIPS + c)],
            hid_s.at[0], hid_r.at[0], {"space": peer},
        ).start()

    each(SPACE, send_hidden)
    each(CHIPS, send_ag)
    do[rows(c, PAIR), :] = ag_tok[:, lanes(c)]
    hbuf[:, lanes(k * CHIPS + c)] = hsend[rows(s, OWN), :]

    flipped = att_tok[...].astype(F32).T.reshape(DP, CHIPS, 2, SLAB, PAIR)
    for core in range(2):
        for zz in range(4):
            for xx in range(4):
                for yy in range(2):
                    rows_of = flipped[yy * 4 + xx, 2 * zz : 2 * zz + 2, core].reshape(16, PAIR)
                    rows_of = rows_of.astype(BF)
                    for path, first_of in enumerate((xx * 4 + zz, zz * 4 + xx)):
                        at = (first_of * 2 + yy) * 16
                        ow_lhs[path, core, at : at + 16, :] = rows_of

    def pass_on(i, carry):
        for path in range(2):
            part = mm(ow_lhs[path, 1 - k, rows(i, PAIR), :], hg_tok[:, path * HALF : path * HALF + HALF])
            ow_pass[path, rows(i, PAIR), :] = part.astype(BF)
        return carry

    lax.fori_loop(0, 4, pass_on, 0)
    ow_copy = remote(ow_pass, ow_in, one_s.at[0], one_r.at[0], partner)
    ow_copy.start()
    def by_x(i):
        dest = lax.rem(along + i, 4)
        return dest, {"dp": across * 4 + dest}

    def by_z(i):
        dest = lax.rem(z + i, 4)
        return dest, {"space": (dest * 2 + column_y) * 2 + k}

    def send_ow(path, way):
        def one(i):
            dest, where = way(i)
            remote(
                ow_send.at[path, rows(dest, PAIR)], ow_recv.at[path, i],
                ow_s.at[path], ow_r.at[path], where,
            ).start()

        each(4, one)

    def sum_ow(path, index):
        take(ow_recv.at[path, pl.ds(1, 3)], ow_r.at[path])
        total = ow_send[path, rows(index, PAIR), :].astype(F32)
        for i in range(1, 4):
            total = total + ow_recv[path, i].astype(F32)
        ow_keep[path] = total
        ow_x[path] = total.astype(BF)

    def send_ow_on(path, way):
        def one(i):
            dest, where = way(i)
            remote(
                ow_x.at[path, rows(dest, GRID)], ow_xr.at[path, i],
                ox_s.at[path], ox_r.at[path], where,
            ).start()

        each(4, one)

    def sum_ow_on(path, index):
        take(ow_xr.at[path, pl.ds(1, 3)], ox_r.at[path])
        total = ow_keep[path, rows(index, GRID), :]
        for i in range(1, 4):
            total = total + ow_xr[path, i].astype(F32)
        ow_y[:, path * HALF : path * HALF + HALF] = total

    for i in range(1, 5):
        for core in range(2):
            take(small, cot_r.at[i, core])
    share(own_blocks, 0)

    ow_copy.wait()

    def join(i, carry):
        for path in range(2):
            part = mm(ow_lhs[path, k, rows(i, PAIR), :], hg_tok[:, path * HALF : path * HALF + HALF])
            both = part + ow_in[path, rows(i, PAIR), :].astype(F32)
            ow_send[path, rows(i, PAIR), :] = both.astype(BF)
        return carry

    lax.fori_loop(0, 4, join, 0)

    send_ow(0, by_x)
    send_ow(1, by_z)

    take(hsend.at[most], hid_r.at[0])

    spot = lax.broadcasted_iota(jnp.int32, (OWN, TOKENS), 1)
    y = lax.shift_right_logical(spot, 5)
    x = spot & (GRID - 1)
    for sample in range(2):
        hidden = hbuf[:, sample * TOKENS : (sample + 1) * TOKENS].astype(F32)
        for row in range(3):
            for col in range(3):
                offset = (row - 1) * GRID + col - 1
                moved = pltpu.roll(hidden, (-offset) % TOKENS, 1) if offset else hidden
                good = None
                for ok in (
                    [y > 0] * (row == 0) + [y < GRID - 1] * (row == 2)
                    + [x > 0] * (col == 0) + [x < GRID - 1] * (col == 2)
                ):
                    good = ok if good is None else good & ok
                if good is not None:
                    moved = jnp.where(good, moved, 0.0)
                tap = 3 * row + col
                lhs[sample, tap * OWN : (tap + 1) * OWN, :] = moved.astype(BF)
        lhs[sample, TAPS * OWN :, :] = jnp.zeros((OWN, TOKENS), BF)
    for j in range(2):
        take(block(0, 0), hop_r.at[j])
    share(hop_blocks, 1)
    mine = rows(k, TOKENS)

    tiles = [(at, min(at + BLOCK, COUT)) for at in range(0, COUT, BLOCK)]
    for at, end in tiles:
        conv_acc[:, at:end] = mm(lhs[k], cot_all[mine, at:end])
    other = rows(1 - k, TOKENS)
    six = cot_all.at[pl.ds(0, 6 * PAIR)]
    two = cot_all.at[pl.ds(0, 2 * PAIR)]
    take(six, share_r.at[0])
    take(two, share_r.at[1])
    for tile, (at, end) in enumerate(tiles):
        part = conv_acc[:, at:end] + mm(lhs[1 - k], cot_all[other, at:end])
        for dest in range(DP):
            for pair in range(5):
                top = pair * 2 * OWN + dest * SLAB
                both = jnp.concatenate(
                    [part[top : top + SLAB], part[top + OWN : top + OWN + SLAB]], axis=0
                )
                conv_send[dest % 4, dest // 4, pair * 16 : pair * 16 + 16, at:end] = both.astype(BF)

        def send_conv(i):
            dest = lax.rem(along + i, 4)
            remote(
                conv_send.at[dest, :, :, at:end], conv_recv.at[i, :, :, at:end],
                conv_s.at[tile], conv_r.at[tile], {"dp": across * 4 + dest},
            ).start()

        each(4, send_conv)

    take(do.at[chips], ag_r.at[0])
    kt[...] = qkv[1].astype(F32).T.astype(BF)
    grad = do[...]
    dom[0] = jnp.where(first, grad, jnp.zeros_like(grad))
    dom[1] = jnp.where(first, jnp.zeros_like(grad), grad)
    dq_acc[...] = jnp.zeros_like(dq_acc)
    product = ot[...].astype(F32) * grad.astype(F32).T
    for h in range(2):
        part = jnp.sum(product[h * HEAD_DIM : (h + 1) * HEAD_DIM], axis=0, keepdims=True)
        delta[h] = jnp.broadcast_to(part, (SLAB, TOKENS))

    def backward(i, carry):
        here = rows(i, BLOCK)
        key_grad = None
        for h in range(2):
            head = slice(h * HEAD_DIM, (h + 1) * HEAD_DIM)
            prob = probs[h, here, :]
            value_part = mm(prob, dom[h])
            prob_grad = mm_nt(qkv[2, here, :], dom[h])
            score_grad = (prob.astype(F32) * (prob_grad - delta[h, 0:1, :])).astype(BF)
            key_part = mm(score_grad, qm[h])
            dq_acc[head, :] += mm(kt[head, here], score_grad)
            key_grad = key_part if key_grad is None else key_grad + key_part
            value_grad = value_part if h == 0 else value_grad + value_part
        gh[1, here, :] = key_grad.astype(BF)
        gh[2, here, :] = value_grad.astype(BF)
        for quarter_of in range(4):
            peer = 4 * i + quarter_of

            @pl.when(peer != s)
            def _():
                remote(
                    gh.at[pl.ds(1, 2), rows(peer, HERE), :],
                    grads_ref.at[pl.ds(1, 2), k, :, lanes(c)],
                    gr_s.at[0], gr_r.at[0], {"space": peer},
                ).start()

        return carry

    lax.fori_loop(0, 2, backward, 0)
    sum_ow(0, along)
    send_ow_on(0, by_z)
    sum_ow(1, z)
    send_ow_on(1, by_x)
    lax.fori_loop(2, TOKENS // BLOCK, backward, 0)
    gh[0] = (dq_acc[...] * SCALE).T.astype(BF)

    def send_query(i):
        peer = to(i)
        remote(
            gh.at[0, rows(peer, HERE), :], grads_ref.at[0, k, :, lanes(c)],
            gq_s.at[0], gq_r.at[0], {"space": peer},
        ).start()

    each(SPACE, send_query)
    own_grads = pltpu.make_async_copy(
        gh.at[:, rows(s, HERE), :], grads_ref.at[:, k, :, lanes(c)], loc.at[0]
    )
    own_grads.start()

    opposite = {"dp": lax.rem(d + 4, DP)}
    turns = []
    for tile, (at, end) in enumerate(tiles):
        take(conv_recv.at[pl.ds(1, 3), :, :, at:end], conv_r.at[tile])
        for half in range(2):
            total = conv_send[along, half, :, at:end].astype(F32)
            for i in range(1, 4):
                total = total + conv_recv[i, half, :, at:end].astype(F32)
            conv_keep[half, :, at:end] = total
        conv_out[:, at:end] = conv_keep[1 - across, :, at:end].astype(BF)
        turn = remote(
            conv_out.at[:, at:end], conv_in.at[:, at:end], cy_s.at[tile], cy_r.at[tile], opposite
        )
        turn.start()
        turns.append(turn)

    sum_ow_on(0, z)
    sum_ow_on(1, along)
    place = across * 2 + column_y

    def send_ow_y(i):
        dest = lax.rem(place + i, 4)
        remote(
            ow_y.at[rows(dest, SLAB)], ow_parts.at[i], oy_s.at[0], oy_r.at[0],
            {"dp": lax.div(dest, 2) * 4 + along, "space": (z * 2 + lax.rem(dest, 2)) * 2 + k},
        ).start()

    each(4, send_ow_y)

    for tile, (at, end) in enumerate(tiles):
        turns[tile].wait()
        total = conv_keep[across, :, at:end] + conv_in[:, at:end].astype(F32)
        for tap in range(TAPS):
            gc_ref[tap, :, at:end] = total[tap * SLAB : (tap + 1) * SLAB]

    take(ow_parts.at[pl.ds(1, 3)], oy_r.at[0])
    total = ow_y[rows(place, SLAB), :]
    for i in range(1, 4):
        total = total + ow_parts[i]
    gw_ref[...] = total

    own_grads.wait()

    take(gh.at[pl.ds(1, 2), most], gr_r.at[0])
    take(gh.at[0, most], gq_r.at[0])
    take(qkv.at[pl.ds(0, 2), most], qkv_s.at[0])
    take(qkv.at[2, most], qkv_s.at[1])
    take(hsend.at[most], hid_s.at[0])
    take(gh.at[pl.ds(1, 2), most], gr_s.at[0])
    take(gh.at[0, most], gq_s.at[0])
    take(att.at[chips], att_s.at[0])
    take(do.at[chips], ag_s.at[0])
    for path in range(2):
        take(ow_recv.at[path, pl.ds(1, 3)], ow_s.at[path])
        take(ow_xr.at[path, pl.ds(1, 3)], ox_s.at[path])
    take(ow_parts.at[pl.ds(1, 3)], oy_s.at[0])
    for tile, (at, end) in enumerate(tiles):
        take(conv_recv.at[pl.ds(1, 3), :, :, at:end], conv_s.at[tile])
    for copy in ring:
        copy.wait_send()
    take(six, share_s.at[0])
    take(two, share_s.at[1])
    for i in range(1, 5):
        for core in range(2):
            take(small, cot_s.at[i, core])
    for core in range(2):
        take(small, near_s.at[core, 1])
    take(small, near_s.at[1 - k, 0])

    @pl.when(((k == 1) & (c < CHIPS - 1)) | ((k == 0) & (c > 0)))
    def _():
        for core in range(2):
            take(cext.at[low_end], halo_s.at[1 + core])


def hand_over(*refs):
    sources, outs, held, sems = refs[:3], refs[3:8], refs[8:13], refs[13]
    grads_ref, gw_ref, gc_ref = sources
    ins = [grads_ref.at[0], grads_ref.at[1], grads_ref.at[2], gw_ref, gc_ref]
    arrive = [pltpu.make_async_copy(a, b, sems.at[0, j]) for j, (a, b) in enumerate(zip(ins, held))]
    leave = [pltpu.make_async_copy(a, b, sems.at[1, j]) for j, (a, b) in enumerate(zip(held, outs))]
    for copy in arrive:
        copy.start()
    for first, second in zip(arrive, leave):
        first.wait()
        second.start()
    for copy in leave:
        copy.wait()


def on_device(queries, keys, values, cotangent, timesteps, time_table, out_weight, conv_weight):
    anywhere = pl.BlockSpec(memory_space=pl.ANY)
    vmem = pl.BlockSpec(memory_space=pltpu.VMEM)
    sems = pltpu.SemaphoreType.DMA
    wide = jax.ShapeDtypeStruct((2, HERE, CH), BF)
    gw_shape = jax.ShapeDtypeStruct((SLAB, CH), F32)
    gc_shape = jax.ShapeDtypeStruct((TAPS, SLAB, COUT), F32)
    parts = pl.pallas_call(
        kernel,
        out_shape=(jax.ShapeDtypeStruct((3, 2, HERE, CH), BF), gw_shape, gc_shape),
        in_specs=[anywhere] * 7 + [pl.BlockSpec(memory_space=pltpu.SMEM)],
        out_specs=(anywhere, vmem, vmem),
        scratch_shapes=[
            pltpu.VMEM((3, TOKENS, PAIR), BF),
            pltpu.VMEM((2 * TOKENS, COUT), BF),
            pltpu.VMEM((PAIR + 2 * GRID, COUT), BF),
            pltpu.VMEM((CH, CH), BF),
            pltpu.VMEM((TAPS, CH, COUT), BF),
            pltpu.VMEM((STEPS, CH), F32),
            pltpu.VMEM((CH, CH), BF),
            pltpu.VMEM((CH, PAIR), F32),
            pltpu.VMEM((2, TOKENS, PAIR), BF),
            pltpu.VMEM((2, TOKENS, PAIR), BF),
            pltpu.VMEM((PAIR, TOKENS), BF),
            pltpu.VMEM((PAIR, TOKENS), BF),
            pltpu.VMEM((2, TOKENS, TOKENS), BF),
            pltpu.VMEM((PAIR, TOKENS), BF),
            pltpu.VMEM((TOKENS, PAIR), BF),
            pltpu.VMEM((PAIR, CH), BF),
            pltpu.VMEM((PAIR, CH), BF),
            pltpu.VMEM((PAIR, CH), BF),
            pltpu.VMEM((CH, PAIR), BF),
            pltpu.VMEM((OWN, 2 * TOKENS), BF),
            pltpu.VMEM((2, 10 * OWN, TOKENS), BF),
            pltpu.VMEM((10 * OWN, COUT), F32),
            pltpu.VMEM((4, 2, ROWS, COUT), BF),
            pltpu.VMEM((4, 2, ROWS, COUT), BF),
            pltpu.VMEM((2, ROWS, COUT), F32),
            pltpu.VMEM((ROWS, COUT), BF),
            pltpu.VMEM((ROWS, COUT), BF),
            pltpu.VMEM((TOKENS, PAIR), BF),
            pltpu.VMEM((2, SLAB, TOKENS), F32),
            pltpu.VMEM((PAIR, TOKENS), F32),
            pltpu.VMEM((3, TOKENS, PAIR), BF),
            pltpu.VMEM((2, 2, HALF, PAIR), BF),
            pltpu.VMEM((2, HALF, HALF), BF),
            pltpu.VMEM((2, HALF, HALF), BF),
            pltpu.VMEM((2, HALF, HALF), BF),
            pltpu.VMEM((2, 4, PAIR, HALF), BF),
            pltpu.VMEM((2, PAIR, HALF), F32),
            pltpu.VMEM((2, PAIR, HALF), BF),
            pltpu.VMEM((2, 4, GRID, HALF), BF),
            pltpu.VMEM((GRID, CH), F32),
            pltpu.VMEM((4, SLAB, CH), F32),
            sems((8,)),
            sems((3,)), sems((3,)),
            sems((2,)), sems((2,)),
            sems((2, 2)), sems((2, 2)),
            sems((5, 2)), sems((5, 2)),
            sems((2,)), sems((2,)),
            sems((2,)), sems((2,)),
            sems((1,)), sems((1,)),
            sems((1,)), sems((1,)),
            sems((1,)), sems((1,)),
            sems((3,)), sems((3,)),
            sems((3,)), sems((3,)),
            sems((2,)), sems((2,)),
            sems((2,)), sems((2,)),
            sems((1,)), sems((1,)),
            sems((1,)), sems((1,)),
            sems((1,)), sems((1,)),
            sems((1,)), sems((1,)),
        ],
        compiler_params=pltpu.CompilerParams(
            collective_id=0, has_side_effects=True, vmem_limit_bytes=60 * 1024 * 1024
        ),
        cost_estimate=pl.CostEstimate(
            flops=8_000_000_000, bytes_accessed=20_000_000, transcendentals=2_000_000
        ),
    )(
        queries, keys, values, cotangent, out_weight, jnp.transpose(conv_weight, (1, 0, 2)),
        time_table, timesteps,
    )
    gq, gk, gv, gw, gc = pl.pallas_call(
        hand_over,
        out_shape=(wide, wide, wide, gw_shape, gc_shape),
        in_specs=[anywhere] * 3,
        out_specs=(anywhere,) * 5,
        scratch_shapes=[pltpu.VMEM((2, HERE, CH), BF)] * 3
        + [pltpu.VMEM((SLAB, CH), F32), pltpu.VMEM((TAPS, SLAB, COUT), F32), sems((2, 5))],
    )(*parts)
    return gq, gk, gv, gw, jnp.transpose(gc, (1, 0, 2))


def solution(mesh):
    return jax.shard_map(
        on_device,
        mesh=mesh,
        in_specs=(
            P("dp", "space", None),
            P("dp", "space", None),
            P("dp", "space", None),
            P("dp", "space", None),
            P("dp"),
            P(),
            P(),
            P(),
        ),
        out_specs=(
            P("dp", "space", None),
            P("dp", "space", None),
            P("dp", "space", None),
            P(("dp", "space"), None),
            P(("dp", "space"), None, None),
        ),
        check_vma=False,
    )
```

```python
import jax
import jax.numpy as jnp
from jax import lax
from jax.experimental import pallas as pl
from jax.experimental.pallas import tpu as pltpu
from jax.sharding import PartitionSpec as P

HEAD_DIM = 64
TAPS = 9
GRID = 32
TOKENS = GRID * GRID
PAIR = 2 * HEAD_DIM
DP = 8
SPACE = 16
CHIPS = 8
CH = 1024
COUT = 640
HERE = 64
SLAB = 8
OWN = DP * SLAB
ROWS = 80
BLOCK = 256
STEPS = 1000
HALF = CH // 2
SCALE = HEAD_DIM ** (-0.5)
MESH = pl.DeviceIdType.MESH
NT = (((1,), (1,)), ((), ()))
BF = jnp.bfloat16
F32 = jnp.float32


def mm(a, b):
    return jnp.dot(a, b, preferred_element_type=F32)


def mm_nt(a, b):
    return lax.dot_general(a, b, NT, preferred_element_type=F32)


def kernel(
    q_ref, k_ref, v_ref, cot_ref, w_ref, wc_ref, table_ref, step_ref,
    grads_ref, gw_ref, gc_ref,
    qkv, cot_all, cext, w, wc, table, wperm, bias_col, qm, dom, vt, kt, probs, ot, att, att_tok,
    hg_tok, ag_tok, hsend, hbuf, lhs, conv_acc, conv_send, conv_recv, conv_keep, conv_out, conv_in, do, delta, dq_acc, gh,
    ow_lhs, ow_pass, ow_in, ow_send, ow_recv, ow_keep, ow_x, ow_xr, ow_y, ow_parts,
    loc, halo_s, halo_r, qkv_s, qkv_r, near_s, near_r, cot_s, cot_r, hop_s, hop_r, share_s, share_r, ag_s, ag_r, att_s, att_r, hid_s, hid_r,
    conv_s, conv_r, cy_s, cy_r, ow_s, ow_r, ox_s, ox_r, oy_s, oy_r, gr_s, gr_r, gq_s, gq_r, one_s, one_r,
):
    d = lax.axis_index("dp")
    s = lax.axis_index("space")
    c = lax.div(s, 2)
    k = lax.rem(s, 2)
    lin = d * 2 + k
    z = lax.div(c, 2)
    column_y = lax.rem(c, 2)
    across = lax.div(d, 4)
    along = lax.rem(d, 4)
    partner = {"space": c * 2 + 1 - k}

    def lanes(chip):
        return pl.ds(pl.multiple_of(chip * PAIR, PAIR), PAIR)

    def rows(index, size):
        return pl.ds(pl.multiple_of(index * size, size), size)

    def to(i):
        return lax.rem(s + i, SPACE)

    def frm(i):
        return lax.rem(s + SPACE - i, SPACE)

    def chip_to(i):
        return lax.rem(c + i, CHIPS)

    def chip_frm(i):
        return lax.rem(c + CHIPS - i, CHIPS)

    def each(count, body):
        def step(i, carry):
            body(i)
            return carry

        lax.fori_loop(1, count, step, 0)

    def take(ref, sem):
        pltpu.make_async_copy(ref, ref, sem).wait()

    def remote(src, dst, send, recv, where):
        return pltpu.make_async_remote_copy(
            src_ref=src, dst_ref=dst, send_sem=send, recv_sem=recv,
            device_id=where, device_id_type=MESH,
        )

    local = [
        pltpu.make_async_copy(w_ref, w, loc.at[0]),
        pltpu.make_async_copy(cot_ref.at[k], cext.at[pl.ds(pl.multiple_of(GRID + k * HERE, GRID), HERE)], loc.at[1]),
        pltpu.make_async_copy(cot_ref.at[k], cot_all.at[rows(k * SPACE + s, HERE)], loc.at[2]),
        pltpu.make_async_copy(q_ref.at[k, :, lanes(c)], qkv.at[0, rows(s, HERE)], loc.at[3]),
        pltpu.make_async_copy(k_ref.at[k, :, lanes(c)], qkv.at[1, rows(s, HERE)], loc.at[4]),
        pltpu.make_async_copy(v_ref.at[k, :, lanes(c)], qkv.at[2, rows(s, HERE)], loc.at[5]),
        pltpu.make_async_copy(table_ref, table, loc.at[6]),
        pltpu.make_async_copy(wc_ref, wc, loc.at[7]),
    ]
    for copy in local:
        copy.start()

    barrier = pltpu.get_barrier_semaphore()

    def greet(i):
        pl.semaphore_signal(barrier, inc=1, device_id={"space": to(i)}, device_id_type=MESH)
        other = lax.rem(lin + i, SPACE)
        pl.semaphore_signal(
            barrier, inc=1,
            device_id={"dp": lax.div(other, 2), "space": c * 2 + lax.rem(other, 2)},
            device_id_type=MESH,
        )

    each(SPACE, greet)
    diagonal = {"dp": lax.rem(d + 4, DP), "space": (z * 2 + 1 - column_y) * 2 + k}
    pl.semaphore_signal(barrier, inc=1, device_id=diagonal, device_id_type=MESH)
    pl.semaphore_wait(barrier, 2 * (SPACE - 1) + 1)

    halo = remote(
        cot_ref.at[1 - k], cext.at[pl.ds(pl.multiple_of(GRID + k * HERE, GRID), HERE)],
        halo_s.at[0], halo_r.at[0], partner,
    )
    halo.start()
    low_end = pl.ds(0, GRID)
    high_end = pl.ds(GRID + PAIR, GRID)

    def edge(core, begin, place, slot, chip):
        return remote(
            cot_ref.at[core, pl.ds(begin, GRID)], cext.at[place],
            halo_s.at[1 + core], halo_r.at[slot], {"space": chip * 2 + core},
        )

    @pl.when((k == 1) & (c < CHIPS - 1))
    def _():
        for core in range(2):
            edge(core, GRID, low_end, 1, c + 1).start()

    @pl.when((k == 0) & (c > 0))
    def _():
        for core in range(2):
            edge(core, 0, high_end, 2, c - 1).start()

    @pl.when(c == 0)
    def _():
        cext[low_end] = jnp.zeros((GRID, COUT), BF)

    @pl.when(c == CHIPS - 1)
    def _():
        cext[high_end] = jnp.zeros((GRID, COUT), BF)

    def send_heads(i, arrays, sem):
        peer = to(i)
        chip = lax.div(peer, 2)
        core = lax.rem(peer, 2)
        for j, ref in arrays:
            remote(
                ref.at[core, :, lanes(chip)], qkv.at[j, rows(s, HERE)],
                qkv_s.at[sem], qkv_r.at[sem], {"space": peer},
            ).start()

    each(SPACE, lambda i: send_heads(i, ((0, q_ref), (1, k_ref)), 0))
    each(SPACE, lambda i: send_heads(i, ((2, v_ref),), 1))

    def near(core, step):
        chip = z * 2 + lax.rem(column_y + step, 2)
        return remote(
            cot_ref.at[core], cot_all.at[rows(core * SPACE + s, HERE)],
            near_s.at[core, step], near_r.at[k, step], {"space": chip * 2 + core},
        )

    for core in range(2):
        near(core, 1).start()

        @pl.when(core != k)
        def _():
            near(core, 0).start()

    for i, (shift_z, shift_y) in enumerate(((1, 0), (3, 0), (2, 0), (2, 1)), 1):
        chip = lax.rem(z + shift_z, 4) * 2 + lax.rem(column_y + shift_y, 2)
        for core in range(2):
            remote(
                cot_ref.at[core], cot_all.at[rows(core * SPACE + s, HERE)],
                cot_s.at[i, core], cot_r.at[i, k], {"space": chip * 2 + core},
            ).start()

    local[0].wait()
    local[6].wait()
    bias_here = table[pl.ds(step_ref[k], 1), :]
    high = bias_here.astype(BF)
    rest = bias_here - high.astype(F32)
    mid = rest.astype(BF)
    low = (rest - mid.astype(F32)).astype(BF)
    pieces = jnp.concatenate(
        [high.astype(F32), mid.astype(F32), low.astype(F32), jnp.zeros((13, CH), F32)], axis=0
    ).astype(BF)

    def permute(i, carry):
        n = lax.broadcasted_iota(jnp.int32, (BLOCK, CH), 0) + i * BLOCK
        e = lax.broadcasted_iota(jnp.int32, (BLOCK, CH), 1)
        n_chip = lax.shift_right_logical(n, 7)
        n_core = lax.shift_right_logical(n, 6) & 1
        n_dp = lax.shift_right_logical(n, 3) & 7
        target = n_dp * 128 + n_chip * 16 + n_core * 8 + (n & 7)
        pick = jnp.where(e == target, 1.0, 0.0).astype(BF)
        wperm[rows(i, BLOCK), :] = mm_nt(pick, w[...]).astype(BF)
        column = jnp.sum(mm_nt(pick, pieces), axis=1, keepdims=True)
        bias_col[rows(i, BLOCK), :] = jnp.broadcast_to(column, (BLOCK, PAIR))
        return carry

    lax.fori_loop(0, CH // BLOCK, permute, 0)

    local[1].wait()
    local[7].wait()
    halo.wait_send()
    take(cext.at[pl.ds(0, HERE)], halo_r.at[0])

    @pl.when(c > 0)
    def _():
        take(cext.at[low_end], halo_r.at[1])

    @pl.when(c < CHIPS - 1)
    def _():
        take(cext.at[high_end], halo_r.at[2])

    sums = []
    for col in range(3):
        total = None
        for row in range(3):
            start = 2 * GRID - GRID * row
            part = mm_nt(cext[start : start + PAIR, :], wc[3 * row + col])
            total = part if total is None else total + part
        sums.append(total)
    column = lax.broadcasted_iota(jnp.int32, (PAIR, CH), 0) & (GRID - 1)
    hidden_grad = (
        sums[1]
        + jnp.where(column < GRID - 1, pltpu.roll(sums[0], PAIR - 1, 0), 0.0)
        + jnp.where(column > 0, pltpu.roll(sums[2], 1, 0), 0.0)
    )
    hg_tok[...] = hidden_grad.astype(BF)
    ag_tok[...] = mm_nt(hg_tok[...], w[...]).astype(BF)

    def send_ag(i):
        chip = chip_to(i)
        remote(
            ag_tok.at[:, lanes(chip)], do.at[rows(c, PAIR)],
            ag_s.at[0], ag_r.at[0], {"space": chip * 2 + k},
        ).start()


    most = pl.ds(0, TOKENS - HERE)
    chips = pl.ds(0, TOKENS - PAIR)
    for copy in local[3:6]:
        copy.wait()
    take(qkv.at[pl.ds(0, 2), most], qkv_r.at[0])

    def block(zz, yy):
        return cot_all.at[pl.ds(pl.multiple_of(k * TOKENS + (zz * 2 + yy) * PAIR, PAIR), PAIR)]

    z_up = lax.rem(z + 1, 4)
    z_down = lax.rem(z + 3, 4)
    z_far = lax.rem(z + 2, 4)
    other_y = 1 - column_y
    small = cot_all.at[pl.ds(0, HERE)]
    ring = []
    for j, (zz, yy, chip) in enumerate((
        (z, other_y, z_up * 2 + column_y),
        (z, other_y, z_down * 2 + column_y),
    )):
        ring.append(
            remote(
                block(zz, yy), block(zz, yy), hop_s.at[j], hop_r.at[j], {"space": chip * 2 + k}
            )
        )
    own_blocks = ((z, 0), (z, 1), (z_up, column_y), (z_down, column_y), (z_far, 0), (z_far, 1))
    hop_blocks = ((z_down, other_y), (z_up, other_y))

    def share(blocks, slot):
        for zz, yy in blocks:
            remote(
                block(zz, yy), block(zz, yy), share_s.at[slot], share_r.at[slot], partner
            ).start()

    first = lax.broadcasted_iota(jnp.int32, (TOKENS, PAIR), 1) < HEAD_DIM
    query = qkv[0] * jnp.asarray(SCALE, BF)
    qm[0] = jnp.where(first, query, jnp.zeros_like(query))
    qm[1] = jnp.where(first, jnp.zeros_like(query), query)

    def weigh(i, carry):
        here = rows(i, BLOCK)
        for h in range(2):
            scores = mm_nt(qkv[1], qm[h, here, :])
            top = jnp.max(scores, axis=0, keepdims=True)
            shifted = jnp.exp(scores - top)
            total = jnp.sum(shifted, axis=0, keepdims=True)
            probs[h, :, here] = (shifted * (1.0 / total)).astype(BF)
        return carry

    lax.fori_loop(0, TOKENS // BLOCK, weigh, 0)
    local[2].wait()
    take(small, near_r.at[1 - k, 0])
    take(small, near_r.at[0, 1])
    take(small, near_r.at[1, 1])
    ring[0].start()
    ring[1].start()
    take(qkv.at[2, most], qkv_r.at[1])
    vt[...] = qkv[2].astype(F32).T.astype(BF)

    def forward(i, carry):
        here = rows(i, BLOCK)
        outs = [
            mm(vt[h * HEAD_DIM : (h + 1) * HEAD_DIM, :], probs[h, :, here]) for h in range(2)
        ]
        out = jnp.concatenate(outs, axis=0)
        ot[:, here] = out.astype(BF)
        att[here, :] = out.T.astype(BF)
        for half in range(2):
            chip = 2 * i + half

            @pl.when(chip != c)
            def _():
                remote(
                    att.at[rows(chip, PAIR)], att_tok.at[:, lanes(c)],
                    att_s.at[0], att_r.at[0], {"space": chip * 2 + k},
                ).start()

        return carry

    lax.fori_loop(0, TOKENS // BLOCK, forward, 0)
    att_tok[:, lanes(c)] = att[rows(c, PAIR), :]

    take(att.at[chips], att_r.at[0])
    hsend[...] = (mm_nt(wperm[...], att_tok[...]) + bias_col[...]).astype(BF)

    def send_hidden(i):
        peer = to(i)
        remote(
            hsend.at[rows(peer, OWN)], hbuf.at[:, lanes(k * CHIPS + c)],
            hid_s.at[0], hid_r.at[0], {"space": peer},
        ).start()

    each(SPACE, send_hidden)
    each(CHIPS, send_ag)
    do[rows(c, PAIR), :] = ag_tok[:, lanes(c)]
    hbuf[:, lanes(k * CHIPS + c)] = hsend[rows(s, OWN), :]

    flipped = att_tok[...].astype(F32).T.reshape(DP, CHIPS, 2, SLAB, PAIR)
    for core in range(2):
        for zz in range(4):
            for xx in range(4):
                for yy in range(2):
                    rows_of = flipped[yy * 4 + xx, 2 * zz : 2 * zz + 2, core].reshape(16, PAIR)
                    rows_of = rows_of.astype(BF)
                    for path, first_of in enumerate((xx * 4 + zz, zz * 4 + xx)):
                        at = (first_of * 2 + yy) * 16
                        ow_lhs[path, core, at : at + 16, :] = rows_of

    def pass_on(i, carry):
        for path in range(2):
            part = mm(ow_lhs[path, 1 - k, rows(i, PAIR), :], hg_tok[:, path * HALF : path * HALF + HALF])
            ow_pass[path, rows(i, PAIR), :] = part.astype(BF)
        return carry

    lax.fori_loop(0, 4, pass_on, 0)
    ow_copy = remote(ow_pass, ow_in, one_s.at[0], one_r.at[0], partner)
    ow_copy.start()
    def by_x(i):
        dest = lax.rem(along + i, 4)
        return dest, {"dp": across * 4 + dest}

    def by_z(i):
        dest = lax.rem(z + i, 4)
        return dest, {"space": (dest * 2 + column_y) * 2 + k}

    def send_ow(path, way):
        def one(i):
            dest, where = way(i)
            remote(
                ow_send.at[path, rows(dest, PAIR)], ow_recv.at[path, i],
                ow_s.at[path], ow_r.at[path], where,
            ).start()

        each(4, one)

    def sum_ow(path, index):
        take(ow_recv.at[path, pl.ds(1, 3)], ow_r.at[path])
        total = ow_send[path, rows(index, PAIR), :].astype(F32)
        for i in range(1, 4):
            total = total + ow_recv[path, i].astype(F32)
        ow_keep[path] = total
        ow_x[path] = total.astype(BF)

    def send_ow_on(path, way):
        def one(i):
            dest, where = way(i)
            remote(
                ow_x.at[path, rows(dest, GRID)], ow_xr.at[path, i],
                ox_s.at[path], ox_r.at[path], where,
            ).start()

        each(4, one)

    def sum_ow_on(path, index):
        take(ow_xr.at[path, pl.ds(1, 3)], ox_r.at[path])
        total = ow_keep[path, rows(index, GRID), :]
        for i in range(1, 4):
            total = total + ow_xr[path, i].astype(F32)
        ow_y[:, path * HALF : path * HALF + HALF] = total

    for i in range(1, 5):
        for core in range(2):
            take(small, cot_r.at[i, core])
    share(own_blocks, 0)

    ow_copy.wait()

    def join(i, carry):
        for path in range(2):
            part = mm(ow_lhs[path, k, rows(i, PAIR), :], hg_tok[:, path * HALF : path * HALF + HALF])
            both = part + ow_in[path, rows(i, PAIR), :].astype(F32)
            ow_send[path, rows(i, PAIR), :] = both.astype(BF)
        return carry

    lax.fori_loop(0, 4, join, 0)

    send_ow(0, by_x)
    send_ow(1, by_z)

    take(hsend.at[most], hid_r.at[0])

    spot = lax.broadcasted_iota(jnp.int32, (OWN, TOKENS), 1)
    y = lax.shift_right_logical(spot, 5)
    x = spot & (GRID - 1)
    for sample in range(2):
        hidden = hbuf[:, sample * TOKENS : (sample + 1) * TOKENS].astype(F32)
        for row in range(3):
            for col in range(3):
                offset = (row - 1) * GRID + col - 1
                moved = pltpu.roll(hidden, (-offset) % TOKENS, 1) if offset else hidden
                good = None
                for ok in (
                    [y > 0] * (row == 0) + [y < GRID - 1] * (row == 2)
                    + [x > 0] * (col == 0) + [x < GRID - 1] * (col == 2)
                ):
                    good = ok if good is None else good & ok
                if good is not None:
                    moved = jnp.where(good, moved, 0.0)
                tap = 3 * row + col
                lhs[sample, tap * OWN : (tap + 1) * OWN, :] = moved.astype(BF)
        lhs[sample, TAPS * OWN :, :] = jnp.zeros((OWN, TOKENS), BF)
    for j in range(2):
        take(block(0, 0), hop_r.at[j])
    share(hop_blocks, 1)
    mine = rows(k, TOKENS)

    tiles = [(at, min(at + BLOCK, COUT)) for at in range(0, COUT, BLOCK)]
    for at, end in tiles:
        conv_acc[:, at:end] = mm(lhs[k], cot_all[mine, at:end])
    other = rows(1 - k, TOKENS)
    six = cot_all.at[pl.ds(0, 6 * PAIR)]
    two = cot_all.at[pl.ds(0, 2 * PAIR)]
    take(six, share_r.at[0])
    take(two, share_r.at[1])
    for tile, (at, end) in enumerate(tiles):
        part = conv_acc[:, at:end] + mm(lhs[1 - k], cot_all[other, at:end])
        for dest in range(DP):
            for pair in range(5):
                top = pair * 2 * OWN + dest * SLAB
                both = jnp.concatenate(
                    [part[top : top + SLAB], part[top + OWN : top + OWN + SLAB]], axis=0
                )
                conv_send[dest % 4, dest // 4, pair * 16 : pair * 16 + 16, at:end] = both.astype(BF)

        def send_conv(i):
            dest = lax.rem(along + i, 4)
            remote(
                conv_send.at[dest, :, :, at:end], conv_recv.at[i, :, :, at:end],
                conv_s.at[tile], conv_r.at[tile], {"dp": across * 4 + dest},
            ).start()

        each(4, send_conv)

    take(do.at[chips], ag_r.at[0])
    kt[...] = qkv[1].astype(F32).T.astype(BF)
    grad = do[...]
    dom[0] = jnp.where(first, grad, jnp.zeros_like(grad))
    dom[1] = jnp.where(first, jnp.zeros_like(grad), grad)
    dq_acc[...] = jnp.zeros_like(dq_acc)
    product = ot[...].astype(F32) * grad.astype(F32).T
    for h in range(2):
        part = jnp.sum(product[h * HEAD_DIM : (h + 1) * HEAD_DIM], axis=0, keepdims=True)
        delta[h] = jnp.broadcast_to(part, (SLAB, TOKENS))

    def backward(i, carry):
        here = rows(i, BLOCK)
        key_grad = None
        for h in range(2):
            head = slice(h * HEAD_DIM, (h + 1) * HEAD_DIM)
            prob = probs[h, here, :]
            value_part = mm(prob, dom[h])
            prob_grad = mm_nt(qkv[2, here, :], dom[h])
            score_grad = (prob.astype(F32) * (prob_grad - delta[h, 0:1, :])).astype(BF)
            key_part = mm(score_grad, qm[h])
            dq_acc[head, :] += mm(kt[head, here], score_grad)
            key_grad = key_part if key_grad is None else key_grad + key_part
            value_grad = value_part if h == 0 else value_grad + value_part
        gh[1, here, :] = key_grad.astype(BF)
        gh[2, here, :] = value_grad.astype(BF)
        for quarter_of in range(4):
            peer = 4 * i + quarter_of

            @pl.when(peer != s)
            def _():
                remote(
                    gh.at[pl.ds(1, 2), rows(peer, HERE), :],
                    grads_ref.at[pl.ds(1, 2), k, :, lanes(c)],
                    gr_s.at[0], gr_r.at[0], {"space": peer},
                ).start()

        return carry

    lax.fori_loop(0, 3, backward, 0)
    sum_ow(0, along)
    send_ow_on(0, by_z)
    sum_ow(1, z)
    send_ow_on(1, by_x)
    lax.fori_loop(3, TOKENS // BLOCK, backward, 0)
    gh[0] = (dq_acc[...] * SCALE).T.astype(BF)

    def send_query(i):
        peer = to(i)
        remote(
            gh.at[0, rows(peer, HERE), :], grads_ref.at[0, k, :, lanes(c)],
            gq_s.at[0], gq_r.at[0], {"space": peer},
        ).start()

    each(SPACE, send_query)
    own_grads = pltpu.make_async_copy(
        gh.at[:, rows(s, HERE), :], grads_ref.at[:, k, :, lanes(c)], loc.at[0]
    )
    own_grads.start()

    opposite = {"dp": lax.rem(d + 4, DP)}
    turns = []
    for tile, (at, end) in enumerate(tiles):
        take(conv_recv.at[pl.ds(1, 3), :, :, at:end], conv_r.at[tile])
        for half in range(2):
            total = conv_send[along, half, :, at:end].astype(F32)
            for i in range(1, 4):
                total = total + conv_recv[i, half, :, at:end].astype(F32)
            conv_keep[half, :, at:end] = total
        conv_out[:, at:end] = conv_keep[1 - across, :, at:end].astype(BF)
        turn = remote(
            conv_out.at[:, at:end], conv_in.at[:, at:end], cy_s.at[tile], cy_r.at[tile], opposite
        )
        turn.start()
        turns.append(turn)

    sum_ow_on(0, z)
    sum_ow_on(1, along)
    place = across * 2 + column_y

    def send_ow_y(i):
        dest = lax.rem(place + i, 4)
        remote(
            ow_y.at[rows(dest, SLAB)], ow_parts.at[i], oy_s.at[0], oy_r.at[0],
            {"dp": lax.div(dest, 2) * 4 + along, "space": (z * 2 + lax.rem(dest, 2)) * 2 + k},
        ).start()

    each(4, send_ow_y)

    for tile, (at, end) in enumerate(tiles):
        turns[tile].wait()
        total = conv_keep[across, :, at:end] + conv_in[:, at:end].astype(F32)
        for tap in range(TAPS):
            gc_ref[tap, :, at:end] = total[tap * SLAB : (tap + 1) * SLAB]

    take(ow_parts.at[pl.ds(1, 3)], oy_r.at[0])
    total = ow_y[rows(place, SLAB), :]
    for i in range(1, 4):
        total = total + ow_parts[i]
    gw_ref[...] = total

    own_grads.wait()

    take(gh.at[pl.ds(1, 2), most], gr_r.at[0])
    take(gh.at[0, most], gq_r.at[0])
    take(qkv.at[pl.ds(0, 2), most], qkv_s.at[0])
    take(qkv.at[2, most], qkv_s.at[1])
    take(hsend.at[most], hid_s.at[0])
    take(gh.at[pl.ds(1, 2), most], gr_s.at[0])
    take(gh.at[0, most], gq_s.at[0])
    take(att.at[chips], att_s.at[0])
    take(do.at[chips], ag_s.at[0])
    for path in range(2):
        take(ow_recv.at[path, pl.ds(1, 3)], ow_s.at[path])
        take(ow_xr.at[path, pl.ds(1, 3)], ox_s.at[path])
    take(ow_parts.at[pl.ds(1, 3)], oy_s.at[0])
    for tile, (at, end) in enumerate(tiles):
        take(conv_recv.at[pl.ds(1, 3), :, :, at:end], conv_s.at[tile])
    for copy in ring:
        copy.wait_send()
    take(six, share_s.at[0])
    take(two, share_s.at[1])
    for i in range(1, 5):
        for core in range(2):
            take(small, cot_s.at[i, core])
    for core in range(2):
        take(small, near_s.at[core, 1])
    take(small, near_s.at[1 - k, 0])

    @pl.when(((k == 1) & (c < CHIPS - 1)) | ((k == 0) & (c > 0)))
    def _():
        for core in range(2):
            take(cext.at[low_end], halo_s.at[1 + core])


def hand_over(*refs):
    sources, outs, held, sems = refs[:3], refs[3:8], refs[8:13], refs[13]
    grads_ref, gw_ref, gc_ref = sources
    ins = [grads_ref.at[0], grads_ref.at[1], grads_ref.at[2], gw_ref, gc_ref]
    arrive = [pltpu.make_async_copy(a, b, sems.at[0, j]) for j, (a, b) in enumerate(zip(ins, held))]
    leave = [pltpu.make_async_copy(a, b, sems.at[1, j]) for j, (a, b) in enumerate(zip(held, outs))]
    for copy in arrive:
        copy.start()
    for first, second in zip(arrive, leave):
        first.wait()
        second.start()
    for copy in leave:
        copy.wait()


def on_device(queries, keys, values, cotangent, timesteps, time_table, out_weight, conv_weight):
    anywhere = pl.BlockSpec(memory_space=pl.ANY)
    vmem = pl.BlockSpec(memory_space=pltpu.VMEM)
    sems = pltpu.SemaphoreType.DMA
    wide = jax.ShapeDtypeStruct((2, HERE, CH), BF)
    gw_shape = jax.ShapeDtypeStruct((SLAB, CH), F32)
    gc_shape = jax.ShapeDtypeStruct((TAPS, SLAB, COUT), F32)
    parts = pl.pallas_call(
        kernel,
        out_shape=(jax.ShapeDtypeStruct((3, 2, HERE, CH), BF), gw_shape, gc_shape),
        in_specs=[anywhere] * 7 + [pl.BlockSpec(memory_space=pltpu.SMEM)],
        out_specs=(anywhere, vmem, vmem),
        scratch_shapes=[
            pltpu.VMEM((3, TOKENS, PAIR), BF),
            pltpu.VMEM((2 * TOKENS, COUT), BF),
            pltpu.VMEM((PAIR + 2 * GRID, COUT), BF),
            pltpu.VMEM((CH, CH), BF),
            pltpu.VMEM((TAPS, CH, COUT), BF),
            pltpu.VMEM((STEPS, CH), F32),
            pltpu.VMEM((CH, CH), BF),
            pltpu.VMEM((CH, PAIR), F32),
            pltpu.VMEM((2, TOKENS, PAIR), BF),
            pltpu.VMEM((2, TOKENS, PAIR), BF),
            pltpu.VMEM((PAIR, TOKENS), BF),
            pltpu.VMEM((PAIR, TOKENS), BF),
            pltpu.VMEM((2, TOKENS, TOKENS), BF),
            pltpu.VMEM((PAIR, TOKENS), BF),
            pltpu.VMEM((TOKENS, PAIR), BF),
            pltpu.VMEM((PAIR, CH), BF),
            pltpu.VMEM((PAIR, CH), BF),
            pltpu.VMEM((PAIR, CH), BF),
            pltpu.VMEM((CH, PAIR), BF),
            pltpu.VMEM((OWN, 2 * TOKENS), BF),
            pltpu.VMEM((2, 10 * OWN, TOKENS), BF),
            pltpu.VMEM((10 * OWN, COUT), F32),
            pltpu.VMEM((4, 2, ROWS, COUT), BF),
            pltpu.VMEM((4, 2, ROWS, COUT), BF),
            pltpu.VMEM((2, ROWS, COUT), F32),
            pltpu.VMEM((ROWS, COUT), BF),
            pltpu.VMEM((ROWS, COUT), BF),
            pltpu.VMEM((TOKENS, PAIR), BF),
            pltpu.VMEM((2, SLAB, TOKENS), F32),
            pltpu.VMEM((PAIR, TOKENS), F32),
            pltpu.VMEM((3, TOKENS, PAIR), BF),
            pltpu.VMEM((2, 2, HALF, PAIR), BF),
            pltpu.VMEM((2, HALF, HALF), BF),
            pltpu.VMEM((2, HALF, HALF), BF),
            pltpu.VMEM((2, HALF, HALF), BF),
            pltpu.VMEM((2, 4, PAIR, HALF), BF),
            pltpu.VMEM((2, PAIR, HALF), F32),
            pltpu.VMEM((2, PAIR, HALF), BF),
            pltpu.VMEM((2, 4, GRID, HALF), BF),
            pltpu.VMEM((GRID, CH), F32),
            pltpu.VMEM((4, SLAB, CH), F32),
            sems((8,)),
            sems((3,)), sems((3,)),
            sems((2,)), sems((2,)),
            sems((2, 2)), sems((2, 2)),
            sems((5, 2)), sems((5, 2)),
            sems((2,)), sems((2,)),
            sems((2,)), sems((2,)),
            sems((1,)), sems((1,)),
            sems((1,)), sems((1,)),
            sems((1,)), sems((1,)),
            sems((3,)), sems((3,)),
            sems((3,)), sems((3,)),
            sems((2,)), sems((2,)),
            sems((2,)), sems((2,)),
            sems((1,)), sems((1,)),
            sems((1,)), sems((1,)),
            sems((1,)), sems((1,)),
            sems((1,)), sems((1,)),
        ],
        compiler_params=pltpu.CompilerParams(
            collective_id=0, has_side_effects=True, vmem_limit_bytes=60 * 1024 * 1024
        ),
        cost_estimate=pl.CostEstimate(
            flops=8_000_000_000, bytes_accessed=20_000_000, transcendentals=2_000_000
        ),
    )(
        queries, keys, values, cotangent, out_weight, jnp.transpose(conv_weight, (1, 0, 2)),
        time_table, timesteps,
    )
    gq, gk, gv, gw, gc = pl.pallas_call(
        hand_over,
        out_shape=(wide, wide, wide, gw_shape, gc_shape),
        in_specs=[anywhere] * 3,
        out_specs=(anywhere,) * 5,
        scratch_shapes=[pltpu.VMEM((2, HERE, CH), BF)] * 3
        + [pltpu.VMEM((SLAB, CH), F32), pltpu.VMEM((TAPS, SLAB, COUT), F32), sems((2, 5))],
    )(*parts)
    return gq, gk, gv, gw, jnp.transpose(gc, (1, 0, 2))


def solution(mesh):
    return jax.shard_map(
        on_device,
        mesh=mesh,
        in_specs=(
            P("dp", "space", None),
            P("dp", "space", None),
            P("dp", "space", None),
            P("dp", "space", None),
            P("dp"),
            P(),
            P(),
            P(),
        ),
        out_specs=(
            P("dp", "space", None),
            P("dp", "space", None),
            P("dp", "space", None),
            P(("dp", "space"), None),
            P(("dp", "space"), None, None),
        ),
        check_vma=False,
    )
```
